32 devices in a mesh: seq: 16 (over z, y, core), head: 2 (over x).
Axes of the slice: x: 2, y: 2, z: 4, core: 2. Of those that a mesh axis runs over, the one named last changes fastest.
Arguments:
- hidden_in: bfloat16 [2048, 2048], P('seq'), may hold values from -6 to 6
- attn_gain: float32 [2048], replicated, may hold values from 0.25 to 1.75
- w_query: bfloat16 [2048, 1024], P(None, 'head'), may hold values from -0.125 to 0.125
- w_key: bfloat16 [2048, 256], P(None, 'head'), may hold values from -0.125 to 0.125
- w_value: bfloat16 [2048, 256], P(None, 'head'), may hold values from -0.125 to 0.125
- query_gain: float32 [64], replicated, may hold values from 1 to 12, as said below
- key_gain: float32 [64], replicated, may hold values from 1 to 12, as said below
- w_output: bfloat16 [1024, 2048], P('head'), may hold values from -0.1875 to 0.1875
- prior_keys: bfloat16 [32, 128, 256], P('seq', None, 'head')
- prior_values: bfloat16 [32, 128, 256], P('seq', None, 'head'), may hold values from -6 to 6
- span_order: int32 [32], replicated, may hold values from 0 to 31, as said below
- key_live: int32 [32], replicated, may hold values 0 or 1
- page_table: int32 [16], replicated, may hold values from 0 to 31, as said below
- page_dest: int32 [16], replicated, may hold values from 0 to 15, as said below
Outputs:
- attn_out: float32 [2048, 2048], P('seq', 'head')
- new_keys: bfloat16 [16, 128, 256], P('seq', None, 'head')
- new_values: bfloat16 [16, 128, 256], P('seq', None, 'head')
The draws below stay inside these ranges and needn't reach their ends.
Inputs may be any that keep to these rules, and one draw needn't show every extreme that they name: span_order holds each block number once. `page_table`: distinct slots; of the 2 slots held by each index of seq (slots i * 2 to i * 2 + 1), exactly 1 are named. `page_dest`: each slot once. `query_gain`: positive. `key_gain`: positive.
All inputs are finite; a program needn't handle non-finite values.
Results may differ from the reference program's by a relative error of at most 0.009.
The reference program's roundings to bfloat16 on the way (of `normed`, `values`, `k_heads` and `attn_heads`) count: a program that leaves them out, or rounds other values in their place, can miss the bound.
Values may be sent and summed in bfloat16 or wider, within the bound.
No kernel may reach another device: no remote copies, remote signals or barrier semaphores. Data moves between devices by JAX's collectives and lax.ppermute only.
A program may use at most 128 MiB of HBM per device.

```python
import math
import jax
import jax.numpy as jnp
from jax import lax

D = 2048
HD = 64
QH = 16
KVH = 4
PAGE = 128
BLOCK = 64
POOL_DEV = 2
SPAN = 2048
NBLK = 32
POOL = 32
PRIOR_PAGES = 16
NEWPAGES = 16


def gain_values(key, salt):
    own_key = jax.random.fold_in(key, salt)
    spread = jnp.exp(jax.random.uniform(own_key, (HD,), jnp.float32, 0.0, math.log(3.0)))
    return spread


def draw_query_gain(key, part):
    return gain_values(key, 1)


def draw_key_gain(key, part):
    return gain_values(key, 2)


def draw_prior_keys(key, part):
    own_key = jax.random.fold_in(key, 3)
    raw_values = jax.random.normal(own_key, (POOL, PAGE, KVH * HD), jnp.float32) * 1.5
    return raw_values.astype(jnp.bfloat16)


def draw_page_table(key, part):
    owners = POOL // POOL_DEV
    scores = jax.random.randint(jax.random.fold_in(key, 5), (owners, POOL_DEV), 0, 1 << 20).astype(jnp.int32)
    lanes = jnp.arange(POOL_DEV, dtype=jnp.int32)
    scores = scores * POOL_DEV + lanes[None, :]
    owner_ids = jnp.arange(owners, dtype=jnp.int32)
    force_first = (owner_ids[:, None] == 0) & (lanes[None, :] == 0)
    force_last = (owner_ids[:, None] == owners - 1) & (lanes[None, :] == POOL_DEV - 1)
    scores = jnp.where(force_first | force_last, -1, scores)
    picked = jnp.argsort(scores, axis=1, stable=True)[:, :POOL_DEV // 2].astype(jnp.int32)
    slots = (owner_ids[:, None] * POOL_DEV + picked).reshape(-1).astype(jnp.int32)
    return jax.random.permutation(jax.random.fold_in(key, 6), slots).astype(jnp.int32)


def order_and_dest(key):
    block_order = jax.random.permutation(jax.random.fold_in(key, 21), jnp.arange(NBLK, dtype=jnp.int32)).astype(jnp.int32)
    base_dest = jax.random.permutation(jax.random.fold_in(key, 22), jnp.arange(NEWPAGES, dtype=jnp.int32)).astype(jnp.int32)
    page_ids = jnp.arange(NEWPAGES, dtype=jnp.int32)
    far_block = jnp.sum(jnp.where(jnp.arange(NBLK, dtype=jnp.int32) == NBLK // 2, block_order, 0)).astype(jnp.int32)
    far_page = (far_block * BLOCK // PAGE).astype(jnp.int32)
    holder = jnp.sum(jnp.where(base_dest == 0, page_ids, 0)).astype(jnp.int32)
    far_slot = jnp.sum(jnp.where(page_ids == far_page, base_dest, 0)).astype(jnp.int32)
    dest = jnp.where(page_ids == far_page, 0, jnp.where(page_ids == holder, far_slot, base_dest)).astype(jnp.int32)
    return (block_order, dest)


def draw_span_order(key, part):
    return order_and_dest(key)[0]


def draw_page_dest(key, part):
    return order_and_dest(key)[1]


def set_ends(values, key, low, top_value):
    shape = values.shape
    spot = [jax.random.randint(jax.random.fold_in(key, axis), (), 0, shape[axis]) for axis in range(len(shape))]
    values = values.at[tuple(spot)].set(low)
    longest = shape.index(max(shape))
    spot[longest] = (spot[longest] + 1) % shape[longest]
    return values.at[tuple(spot)].set(top_value)


def shard_levels(stream_key, extent, cuts, smallest, largest):
    def one(dim, shards_of):
        heights = jax.random.uniform(jax.random.fold_in(jax.random.fold_in(stream_key, 6), dim), (shards_of,), jnp.float32, smallest / len(cuts), largest / len(cuts))
        return jnp.repeat(jnp.exp(heights), extent[dim] // shards_of).reshape((-1,) + (1,) * (len(extent) - dim - 1))

    loudness = one(*cuts[0])
    for cut in cuts[1:]:
        loudness = loudness * one(*cut)
    return loudness


def centred(key, extent, deviation, limit, pieces=(), kind=jnp.bfloat16):
    level = shard_levels(key, extent, pieces, -0.22, 0.18) if pieces else 1.0
    drawn = jax.random.normal(key, extent, jnp.float32) * deviation * level
    return jnp.minimum(jnp.maximum(drawn, -limit), limit).astype(kind)


def setup_inputs(seed: int = 0) -> dict:
    keys = jax.random.split(jax.random.key(seed), 15)
    return {
        "hidden_in": centred(keys[0], (SPAN, D), 1.0, 6.0, ((0, 16),)),
        "attn_gain": jnp.clip(1.0 + 0.15 * jax.random.normal(keys[1], (D,), jnp.float32), 0.25, 1.75),
        "w_query": centred(keys[2], (D, QH * HD), D ** -0.5, 0.125, ((1, 2),)),
        "w_key": centred(keys[3], (D, KVH * HD), D ** -0.5, 0.125, ((1, 2),)),
        "w_value": centred(keys[4], (D, KVH * HD), D ** -0.5, 0.125, ((1, 2),)),
        "query_gain": draw_query_gain(jax.random.fold_in(keys[14], 71), 0),
        "key_gain": draw_key_gain(jax.random.fold_in(keys[14], 71), 0),
        "w_output": centred(keys[7], (QH * HD, D), (QH * HD) ** -0.5, 0.1875, ((0, 2),)),
        "prior_keys": draw_prior_keys(jax.random.fold_in(keys[14], 71), 0),
        "prior_values": centred(keys[9], (POOL, PAGE, KVH * HD), 1.0, 6.0, ((0, 16), (2, 2))),
        "span_order": draw_span_order(jax.random.fold_in(keys[14], 71), 0),
        "key_live": set_ends((jax.random.randint(keys[11], (NBLK,), 0, 4) < 3).astype(jnp.int32), jax.random.fold_in(keys[11], 1), 0, 1),
        "page_table": draw_page_table(jax.random.fold_in(keys[14], 71), 0),
        "page_dest": draw_page_dest(jax.random.fold_in(keys[14], 71), 0),
    }


epsilon = 1e-06

def head_norm(vectors, channel_gain):
    mean_square = lax.optimization_barrier(jnp.mean(vectors * vectors, axis=-1, keepdims=True))
    return vectors * lax.rsqrt(mean_square + epsilon) * channel_gain

def rotary(vectors, positions):
    half_dim = vectors.shape[-1] // 2
    lanes = jnp.arange(half_dim, dtype=jnp.float32)
    inverse_freq = jnp.power(10000.0, -lanes / half_dim)
    angles = positions.astype(jnp.float32)[:, None] * inverse_freq[None, :]
    cosine = jnp.cos(angles)[:, None, :]
    sine_part = jnp.sin(angles)[:, None, :]
    first_half = vectors[..., :half_dim]
    second_half = vectors[..., half_dim:]
    return jnp.concatenate([first_half * cosine - second_half * sine_part, second_half * cosine + first_half * sine_part], axis=-1)

def reference(hidden_in, attn_gain, w_query, w_key, w_value, query_gain, key_gain, w_output, prior_keys, prior_values, span_order, key_live, page_table, page_dest):
    prior_len = PRIOR_PAGES * PAGE
    row_index = jnp.arange(SPAN, dtype=jnp.int32)
    logical = span_order[row_index // BLOCK]
    positions = (prior_len + logical * BLOCK + row_index % BLOCK).astype(jnp.int32)
    widened = hidden_in.astype(jnp.float32)
    normed = (widened * lax.rsqrt(lax.optimization_barrier(jnp.mean(widened * widened, axis=-1, keepdims=True)) + epsilon) * attn_gain).astype(jnp.bfloat16)
    queries = jnp.dot(normed, w_query, preferred_element_type=jnp.float32)
    keys_raw = jnp.dot(normed, w_key, preferred_element_type=jnp.float32)
    values = jnp.dot(normed, w_value, preferred_element_type=jnp.float32).astype(jnp.bfloat16)
    q_heads = rotary(head_norm(queries.reshape(SPAN, QH, HD), query_gain), positions) * HD ** (-0.5)
    k_heads = rotary(head_norm(keys_raw.reshape(SPAN, KVH, HD), key_gain), positions).astype(jnp.bfloat16)
    prior_k = prior_keys[page_table].reshape(prior_len, KVH, HD)
    prior_v = prior_values[page_table].reshape(prior_len, KVH, HD)
    all_keys = jnp.concatenate([prior_k, k_heads], axis=0).astype(jnp.float32)
    all_values = jnp.concatenate([prior_v, values.reshape(SPAN, KVH, HD)], axis=0).astype(jnp.float32)
    key_pos = jnp.concatenate([jnp.full((prior_len,), -1, jnp.int32), positions])
    key_ok = jnp.concatenate([jnp.ones((prior_len,), dtype=bool), key_live[logical] > 0])
    group = QH // KVH
    query_block = 256 if SPAN % 256 == 0 else SPAN
    outputs = []
    for head_index in range(KVH):
        query_group = q_heads[:, head_index * group:(head_index + 1) * group, :]
        key_head = all_keys[:, head_index, :]
        value_head = all_values[:, head_index, :]

        def one_block(items):
            query_rows, query_pos = items
            scores = jnp.einsum('qgd,kd->qgk', query_rows, key_head, precision=lax.Precision.HIGHEST)
            allowed = key_ok[None, :] & (key_pos[None, :] <= query_pos[:, None])
            scores = jnp.where(allowed[:, None, :], scores, -jnp.inf)
            highest = lax.optimization_barrier(jnp.max(scores, axis=-1, keepdims=True))
            weights = jnp.where(allowed[:, None, :], jnp.exp(scores - highest), 0.0)
            mixed = jnp.einsum('qgk,kd->qgd', weights, value_head, precision=lax.Precision.HIGHEST)
            return mixed / lax.optimization_barrier(jnp.sum(weights, axis=-1, keepdims=True))
        blocked = lax.map(one_block, (query_group.reshape(-1, query_block, group, HD), positions.reshape(-1, query_block)))
        outputs.append(blocked.reshape(SPAN, group, HD))
    attn_heads = jnp.concatenate(outputs, axis=1).reshape(SPAN, QH * HD).astype(jnp.bfloat16)
    attn_out = jnp.dot(attn_heads, w_output, preferred_element_type=jnp.float32)
    logical_rows = (positions - prior_len).astype(jnp.int32)
    logical_k = jnp.zeros((SPAN, KVH * HD), jnp.bfloat16).at[logical_rows].set(k_heads.reshape(SPAN, KVH * HD))
    logical_v = jnp.zeros((SPAN, KVH * HD), jnp.bfloat16).at[logical_rows].set(values)
    new_keys = jnp.zeros((NEWPAGES, PAGE, KVH * HD), jnp.bfloat16).at[page_dest].set(logical_k.reshape(NEWPAGES, PAGE, KVH * HD))
    new_values = jnp.zeros((NEWPAGES, PAGE, KVH * HD), jnp.bfloat16).at[page_dest].set(logical_v.reshape(NEWPAGES, PAGE, KVH * HD))
    return (attn_out, new_keys, new_values)
```

```python
import functools

import jax
import jax.numpy as jnp
import numpy as np
from jax import lax
from jax.experimental import pallas as pl
from jax.experimental.pallas import tpu as pltpu
from jax.sharding import PartitionSpec as P

PAGE = 128
BLOCK = 64
EPS = 1e-06
MASKED = -1e30
F32 = jnp.float32
BF16 = jnp.bfloat16
VMEM = pltpu.VMEM
SMEM = pltpu.SMEM
LOG2E = 1.4426950408889634


def spec(space):
    return pl.BlockSpec(memory_space=space)


def params(mib=32):
    return pltpu.CompilerParams(vmem_limit_bytes=mib * 1024 * 1024)


def cost(flops, size):
    return pl.CostEstimate(flops=int(flops), bytes_accessed=int(size), transcendentals=0)


def lanes_of(shape):
    return lax.broadcasted_iota(jnp.int32, shape, len(shape) - 1)


def select_kernel(table, prior_keys, prior_values, out, sems):
    first = lax.axis_index("seq") * prior_keys.shape[0]

    def look(i, found):
        slot = table[i] - first
        return jnp.where((slot >= 0) & (slot < prior_keys.shape[0]), slot, found)

    slot = lax.fori_loop(0, table.shape[0], look, 0)
    width = prior_keys.shape[-1]
    copies = [
        pltpu.make_async_copy(prior_keys.at[slot], out.at[:, :width], sems.at[0]),
        pltpu.make_async_copy(prior_values.at[slot], out.at[:, width:], sems.at[1]),
    ]
    for copy in copies:
        copy.start()
    for copy in copies:
        copy.wait()


def norm_and_rotate(x, gain, cosine, sine):
    lane = lanes_of(x.shape)
    left = lane < 64
    square = x * x
    sum_left = jnp.sum(jnp.where(left, square, 0.0), axis=-1, keepdims=True)
    sum_right = jnp.sum(jnp.where(left, 0.0, square), axis=-1, keepdims=True)
    mean = jnp.where(left, sum_left, sum_right) * (1.0 / 64)
    y = x * lax.rsqrt(mean + EPS) * gain
    swapped = jnp.where(lane % 64 < 32, pltpu.roll(y, 96, 1), pltpu.roll(y, 32, 1))
    return y * cosine + swapped * sine


def twice(gain_ref):
    gain = gain_ref[...]
    return jnp.concatenate([gain, gain], axis=-1)


def kv_kernel(
    prior_len, order, hidden, gain, w_key, w_value, key_gain, freq, kv, normed_out, cos_out, sin_out
):
    rows = hidden.shape[0]
    blocks = rows // BLOCK
    me = lax.axis_index("seq")
    wide = hidden[...].astype(F32)
    mean = jnp.mean(wide * wide, axis=-1, keepdims=True)
    normed = (wide * lax.rsqrt(mean + EPS) * gain[...]).astype(BF16)
    normed_out[...] = normed
    values = jnp.dot(normed, w_value[...], preferred_element_type=F32)
    keys = jnp.dot(normed, w_key[...], preferred_element_type=F32)
    row = lax.broadcasted_iota(jnp.int32, (BLOCK, 128), 0)
    lane = lanes_of((BLOCK, 128))
    for b in range(blocks):
        base = prior_len + order[me * blocks + b] * BLOCK
        angle = (base + row).astype(F32) * freq[...]
        part = pl.ds(b * BLOCK, BLOCK)
        sine = jnp.sin(angle)
        cos_out[part, :] = jnp.cos(angle)
        sin_out[part, :] = jnp.where(lane % 64 < 32, -sine, sine)
    rotated = norm_and_rotate(keys, twice(key_gain), cos_out[...], sin_out[...])
    kv[:, :128] = rotated.astype(BF16)
    kv[:, 128:] = values.astype(BF16)


def query_kernel(normed, w_query, query_gain, cosine, sine, q_out):
    rows = normed.shape[0]
    blocks = rows // BLOCK
    tiles = w_query.shape[1] // 128
    per_kv = tiles // 2
    group = 2 * per_kv
    queries = jnp.dot(normed[...], w_query[...], preferred_element_type=F32)
    gain = twice(query_gain)
    left = lanes_of((rows, 128)) < 64
    for t in range(tiles):
        kv_head, u = divmod(t, per_kv)
        x = norm_and_rotate(queries[:, t * 128 : (t + 1) * 128], gain, cosine[...], sine[...])
        x = x * (64**-0.5 * LOG2E)
        turned = pltpu.roll(x, 64, 1)
        pair = (x, turned) if kv_head == 0 else (turned, x)
        for odd, head in enumerate(pair):
            kept = jnp.where(left if kv_head == 0 else ~left, head, 0.0)
            high = kept.astype(BF16)
            low = (kept - high.astype(F32)).astype(BF16)
            both = jnp.concatenate([high, low], axis=-1)
            for b in range(blocks):
                at = ((kv_head * blocks + b) * group + 2 * u + odd) * BLOCK
                q_out[at : at + BLOCK, :] = both[b * BLOCK : (b + 1) * BLOCK, :]


def fold(q, kv_rows, bias, kv_head, m_old, acc_old):
    keys = kv_rows[:, :128]
    values = kv_rows[:, 128:]
    scores = lax.dot_general(
        q,
        jnp.concatenate([keys, keys], axis=-1),
        (((1,), (1,)), ((), ())),
        preferred_element_type=F32,
    )
    if bias is not None:
        scores = scores + bias
    left = lanes_of(values.shape) < 64
    mine = left if kv_head == 0 else ~left
    extended = jnp.where(mine, values, jnp.ones_like(values))
    m_new = jnp.max(scores, axis=-1, keepdims=True)
    if m_old is not None:
        m_new = jnp.maximum(m_old, m_new)
    weights = jnp.exp2(scores - m_new).astype(BF16)
    acc = jnp.dot(weights, extended, preferred_element_type=F32)
    if m_old is not None:
        acc = acc + acc_old * jnp.exp2(m_old - m_new)
    return m_new, acc


def attention_kernel(
    n_chunks, own, first, last, step, blocks, group, chunk_slots, *refs
):
    refs = list(refs)
    q = refs.pop(0)
    if own:
        own_kv = refs.pop(0)
    chunks = [refs.pop(0) for _ in range(n_chunks)]
    order, live = refs.pop(0), refs.pop(0)
    masked = chunk_slots is not None
    if masked:
        slots_ref = refs.pop(0)
    if not first:
        m_in, acc_in = refs.pop(0), refs.pop(0)
    if last:
        out = refs.pop(0)
    m_ref, acc_ref = refs.pop(0), refs.pop(0)
    held, sems = refs.pop(0), refs.pop(0)
    me = lax.axis_index("seq")

    copies = []
    at = 0
    for i, chunk in enumerate(chunks):
        size = chunk.shape[0]
        copies.append(pltpu.make_async_copy(chunk, held.at[pl.ds(at, size)], sems.at[i]))
        at += size
    for copy in copies:
        copy.start()

    part = group * BLOCK
    tiles = 2 * blocks
    q_logical = [order[me * blocks + b] for b in range(blocks)]
    if own:
        total = blocks * BLOCK
        key_at = lanes_of((part, total))
        row = lax.broadcasted_iota(jnp.int32, (part, total), 0) % BLOCK
        for tile in range(tiles):
            kv_head, b = divmod(tile, blocks)
            bias = jnp.full((part, total), MASKED, F32)
            for kb in range(blocks):
                alive = live[q_logical[kb]] > 0
                before = (q_logical[kb] < q_logical[b]) & alive
                here = key_at // BLOCK == kb
                if kb == b:
                    allowed = here & (key_at % BLOCK <= row)
                    bias = jnp.where(allowed, jnp.where(alive, 0.0, MASKED), bias)
                else:
                    bias = jnp.where(here, jnp.where(before, 0.0, MASKED), bias)
            rows = pl.ds(tile * part, part)
            m, acc = fold(q[rows, :], own_kv[...], bias, kv_head, None, None)
            m_ref[rows, :] = jnp.broadcast_to(m, (part, 128))
            acc_ref[rows, :] = acc
    for copy in copies:
        copy.wait()

    n_steps = at // step
    for_loop_started = own

    def visit(c, started):
        key_rows = held[pl.ds(pl.multiple_of(c * step, step), step), :]
        if masked:
            biases = []
            lane = lanes_of((1, 128))
            for b in range(blocks):
                pieces = []
                for s in range(step // 128):
                    rank = me ^ slots_ref[me % 2, chunk_slots + c * (step // 128) + s]
                    value = []
                    for half in range(2):
                        logical = order[rank * 2 + half]
                        fine = (live[logical] > 0) & (logical < q_logical[b]) & (rank != me)
                        value.append(jnp.where(fine, 0.0, MASKED))
                    pieces.append(jnp.where(lane < 64, value[0], value[1]))
                biases.append(jnp.concatenate(pieces, axis=-1))
        for tile in range(tiles):
            kv_head, b = divmod(tile, blocks)
            rows = pl.ds(tile * part, part)
            if started:
                m_old, acc_old = m_ref[rows, :1], acc_ref[rows, :]
            elif not first:
                m_old, acc_old = m_in[rows, :1], acc_in[rows, :]
            else:
                m_old = acc_old = None
            bias = biases[b] if masked else None
            m, acc = fold(q[rows, :], key_rows, bias, kv_head, m_old, acc_old)
            m_ref[rows, :] = jnp.broadcast_to(m, (part, 128))
            acc_ref[rows, :] = acc

    visit(0, for_loop_started)
    if n_steps > 1:
        pl.loop(1, n_steps)(lambda c: visit(c, True))

    if last:
        left = lanes_of((BLOCK, 128)) < 64
        for kv_head in range(2):
            for b in range(blocks):
                for u in range(group // 2):
                    heads = []
                    for odd in range(2):
                        at = ((kv_head * blocks + b) * group + 2 * u + odd) * BLOCK
                        acc = acc_ref[at : at + BLOCK, :]
                        turned = pltpu.roll(acc, 64, 1)
                        ratio = acc / turned
                        heads.append(pltpu.roll(ratio, 64, 1) if odd != kv_head else ratio)
                    both = jnp.where(left, heads[0], heads[1]).astype(BF16)
                    tile = kv_head * (group // 2) + u
                    out[b * BLOCK : (b + 1) * BLOCK, tile * 128 : (tile + 1) * 128] = both


def attention(q, own_kv, chunks, order, live, slots, state, last, chunk_slots, step, blocks, group):
    own = own_kv is not None
    rows = sum(c.shape[0] for c in chunks)
    step = min(step, rows)
    first = state is None
    operands = [q] + ([own_kv] if own else []) + list(chunks) + [order, live]
    specs = [spec(VMEM)] + ([spec(VMEM)] if own else []) + [spec(pl.ANY)] * len(chunks)
    specs += [spec(SMEM), spec(SMEM)]
    if chunk_slots is not None:
        operands.append(slots)
        specs.append(spec(SMEM))
    if not first:
        operands += list(state)
        specs += [spec(VMEM)] * 2
    n = q.shape[0]
    pair = [jax.ShapeDtypeStruct((n, 128), F32)] * 2
    scratch = [VMEM((rows, 256), BF16), pltpu.SemaphoreType.DMA((len(chunks),))]
    if last:
        outs = jax.ShapeDtypeStruct((blocks * BLOCK, 2 * group * 64), BF16)
        out_specs = spec(VMEM)
        scratch = [VMEM((n, 128), F32)] * 2 + scratch
    else:
        outs, out_specs = pair, [spec(VMEM)] * 2
    return pl.pallas_call(
        functools.partial(
            attention_kernel, len(chunks), own, first, last, step, blocks, group, chunk_slots
        ),
        out_shape=outs,
        in_specs=specs,
        out_specs=out_specs,
        scratch_shapes=scratch,
        compiler_params=params(48),
        cost_estimate=cost(4 * n * rows * 256, rows * 512 + n * 2048),
    )(*operands)


def pages_kernel(n_chunks, dest, order, where, *refs):
    chunks, (keys, values, sems) = refs[:n_chunks], refs[n_chunks:]
    me = lax.axis_index("seq")

    def find(table):
        def body(wanted):
            return lax.fori_loop(
                0, table.shape[0], lambda i, f: jnp.where(table[i] == wanted, i, f), 0
            )

        return body

    page = find(dest)(me)
    for half in range(2):
        source = find(order)(page * 2 + half)
        slot = where[me % 2, me ^ (source // 2)]
        row = slot * PAGE + (source % 2) * BLOCK
        at = 0
        for chunk in chunks:
            size = chunk.shape[0]
            inside = (row >= at) & (row < at + size)

            @pl.when(inside)
            def _(chunk=chunk, at=at):
                rows = pl.ds(pl.multiple_of(row - at, BLOCK), BLOCK)
                to = pl.ds(half * BLOCK, BLOCK)
                a = pltpu.make_async_copy(chunk.at[rows, :128], keys.at[0, to], sems.at[0])
                b = pltpu.make_async_copy(chunk.at[rows, 128:], values.at[0, to], sems.at[1])
                a.start()
                b.start()
                a.wait()
                b.wait()

            at += size


def project_kernel(mine, peer, w_mine_all, w_peer, out, w_mine, sem):
    width = out.shape[1]
    x = lax.axis_index("head")
    columns = pl.ds(pl.multiple_of(x * width, width), width)
    copy = pltpu.make_async_copy(w_mine_all.at[:, columns], w_mine, sem)
    copy.start()
    total = jnp.dot(peer[...], w_peer[...], preferred_element_type=F32)
    copy.wait()
    out[...] = total + jnp.dot(mine[...], w_mine[...], preferred_element_type=F32)


def plan(n):
    bits = [1 << i for i in range(1, n.bit_length() - 1)]
    down = bits[::-1]
    even = down
    odd = [down[-1]] + down[:-1] if len(down) > 1 else down
    return [list(pair) for pair in zip(even, odd)]


def slot_masks(steps):
    masks = []
    for parity in range(2):
        held = [0]
        for step in steps:
            held = held + [m ^ step[parity] for m in held]
        masks.append(held)
    full = [masks[p] + [m ^ 1 for m in masks[1 - p]] for p in range(2)]
    return np.array(full, np.int32)


def swap(x, n, step):
    return lax.ppermute(x, "seq", [(i, i ^ step[i & 1]) for i in range(n)])


def spread(own, n, steps):
    first = swap(own, n, steps[0])
    near = jnp.concatenate([own, first], axis=0)
    chunks = [near]
    for step in steps[1:]:
        chunks = chunks + [swap(c, n, step) for c in chunks]
    other = [swap(c, n, [1, 1]) for c in chunks]
    return chunks, other


def body(
    n,
    hidden_in,
    attn_gain,
    w_query,
    w_key,
    w_value,
    query_gain,
    key_gain,
    w_output,
    prior_keys,
    prior_values,
    span_order,
    key_live,
    page_table,
    page_dest,
):
    rows, width = hidden_in.shape
    blocks = rows // BLOCK
    head_dim = query_gain.shape[0]
    group = w_query.shape[1] // w_key.shape[1]
    prior_len = page_table.shape[0] * PAGE
    steps = plan(n)
    masks = slot_masks(steps)
    where = np.zeros_like(masks)
    for p in range(2):
        where[p, masks[p]] = np.arange(n)
    half = head_dim // 2
    freq = np.tile((10000.0 ** (-np.arange(half) / half)).astype(np.float32), 4)[None, :]
    slots = jnp.asarray(masks)

    prior = pl.pallas_call(
        select_kernel,
        out_shape=jax.ShapeDtypeStruct((PAGE, 256), BF16),
        in_specs=[spec(SMEM), spec(pl.ANY), spec(pl.ANY)],
        out_specs=spec(VMEM),
        scratch_shapes=[pltpu.SemaphoreType.DMA((2,))],
        compiler_params=params(),
        cost_estimate=cost(1000, 1 << 17),
    )(page_table, prior_keys, prior_values)

    kv, normed, cosine, sine = pl.pallas_call(
        functools.partial(kv_kernel, prior_len),
        out_shape=[
            jax.ShapeDtypeStruct((rows, 256), BF16),
            jax.ShapeDtypeStruct((rows, width), BF16),
            jax.ShapeDtypeStruct((rows, 128), F32),
            jax.ShapeDtypeStruct((rows, 128), F32),
        ],
        in_specs=[spec(SMEM)] + [spec(VMEM)] * 6,
        out_specs=[spec(VMEM)] * 4,
        compiler_params=params(),
        cost_estimate=cost(2 * rows * width * 256, 3 << 20),
    )(
        span_order,
        hidden_in,
        attn_gain.reshape(1, -1),
        w_key,
        w_value,
        key_gain.reshape(1, -1),
        jnp.asarray(freq),
    )

    prior_same, prior_other = spread(prior, n, steps)
    span_same, span_other = spread(kv, n, steps)

    x = lax.axis_index("head")
    out_width = w_output.shape[1] // 2
    w_send = lax.dynamic_slice_in_dim(w_output, (1 - x) * out_width, out_width, 1)
    w_peer = lax.ppermute(w_send, "head", [(0, 1), (1, 0)])

    q = pl.pallas_call(
        query_kernel,
        out_shape=jax.ShapeDtypeStruct((2 * blocks * group * BLOCK, 256), BF16),
        in_specs=[spec(VMEM)] * 5,
        out_specs=spec(VMEM),
        compiler_params=params(),
        cost_estimate=cost(2 * rows * width * 512, 4 << 20),
    )(normed, w_query, query_gain.reshape(1, -1), cosine, sine)

    common = dict(order=span_order, live=key_live, slots=slots, blocks=blocks, group=group)
    state = attention(
        q, kv, prior_same + prior_other, state=None, last=False, chunk_slots=None, step=1024, **common
    )
    state = attention(
        q, None, span_same, state=state, last=False, chunk_slots=0, step=1024, **common
    )
    heads = attention(
        q, None, span_other, state=state, last=True, chunk_slots=n // 2, step=1024, **common
    )
    peer = lax.ppermute(heads, "head", [(0, 1), (1, 0)])

    all_span = span_same + span_other
    new_keys, new_values = pl.pallas_call(
        functools.partial(pages_kernel, len(all_span)),
        out_shape=[jax.ShapeDtypeStruct((1, PAGE, 128), BF16)] * 2,
        in_specs=[spec(SMEM)] * 3 + [spec(pl.ANY)] * len(all_span),
        out_specs=[spec(VMEM)] * 2,
        scratch_shapes=[pltpu.SemaphoreType.DMA((2,))],
        compiler_params=params(),
        cost_estimate=cost(1000, 1 << 18),
    )(page_dest, span_order, jnp.asarray(where), *all_span)

    attn_out = pl.pallas_call(
        project_kernel,
        out_shape=jax.ShapeDtypeStruct((rows, out_width), F32),
        in_specs=[spec(VMEM), spec(VMEM), spec(pl.ANY), spec(VMEM)],
        out_specs=spec(VMEM),
        scratch_shapes=[VMEM((w_output.shape[0], out_width), BF16), pltpu.SemaphoreType.DMA],
        compiler_params=params(),
        cost_estimate=cost(4 * rows * 512 * out_width, 4 << 20),
    )(heads, peer, w_output, w_peer)
    return attn_out, new_keys, new_values


def solution(mesh):
    return jax.shard_map(
        functools.partial(body, mesh.shape["seq"]),
        mesh=mesh,
        in_specs=(
            P("seq", None),
            P(),
            P(None, "head"),
            P(None, "head"),
            P(None, "head"),
            P(),
            P(),
            P("head", None),
            P("seq", None, "head"),
            P("seq", None, "head"),
            P(),
            P(),
            P(),
            P(),
        ),
        out_specs=(P("seq", "head"), P("seq", None, "head"), P("seq", None, "head")),
        check_vma=False,
    )
```

```python
import functools

import jax
import jax.numpy as jnp
import numpy as np
from jax import lax
from jax.experimental import pallas as pl
from jax.experimental.pallas import tpu as pltpu
from jax.sharding import PartitionSpec as P

PAGE = 128
BLOCK = 64
EPS = 1e-06
MASKED = -1e30
F32 = jnp.float32
BF16 = jnp.bfloat16
VMEM = pltpu.VMEM
SMEM = pltpu.SMEM
LOG2E = 1.4426950408889634


def spec(space):
    return pl.BlockSpec(memory_space=space)


def in_hbm(*arrays):
    return [pltpu.with_memory_space_constraint(a, pltpu.HBM) for a in arrays]


def params(mib=32):
    return pltpu.CompilerParams(vmem_limit_bytes=mib * 1024 * 1024)


def cost(flops, size):
    return pl.CostEstimate(flops=int(flops), bytes_accessed=int(size), transcendentals=0)


def lanes_of(shape):
    return lax.broadcasted_iota(jnp.int32, shape, len(shape) - 1)


def norm_and_rotate(x, gain, cosine, sine):
    lane = lanes_of(x.shape)
    left = lane < 64
    square = x * x
    sum_left = jnp.sum(jnp.where(left, square, 0.0), axis=-1, keepdims=True)
    sum_right = jnp.sum(jnp.where(left, 0.0, square), axis=-1, keepdims=True)
    mean = jnp.where(left, sum_left, sum_right) * (1.0 / 64)
    y = x * lax.rsqrt(mean + EPS) * gain
    swapped = jnp.where(lane % 64 < 32, pltpu.roll(y, 96, 1), pltpu.roll(y, 32, 1))
    return y * cosine + swapped * sine


def twice(gain_ref):
    gain = gain_ref[...]
    return jnp.concatenate([gain, gain], axis=-1)


def kv_kernel(
    prior_len, order, table, hidden, gain, w_key, w_value, key_gain, freq, prior_keys, prior_values,
    w_query, w_output,
    kv, prior, normed_out, cos_out, sin_out, w_query_out, w_send,
    order_s, table_s, hidden_v, gain_v, w_key_v, w_value_v, key_gain_v, freq_v, sems,
):
    rows = hidden.shape[0]
    blocks = rows // BLOCK
    me = lax.axis_index("seq")
    pairs = [
        (table, table_s), (order, order_s), (freq, freq_v), (key_gain, key_gain_v),
        (gain, gain_v), (hidden, hidden_v), (w_key, w_key_v), (w_value, w_value_v),
    ]
    copies = [pltpu.make_async_copy(a, b, sems.at[i]) for i, (a, b) in enumerate(pairs)]
    later = [
        pltpu.make_async_copy(w_query, w_query_out, sems.at[10]),
        pltpu.make_async_copy(
            w_output.at[half_rows(w_send, me % 2), columns(w_send, 1)], w_send, sems.at[11]
        ),
    ]
    for copy in copies + later:
        copy.start()
    copies[0].wait()
    first = me * prior_keys.shape[0]

    def look(i, found):
        slot = table_s[i] - first
        return jnp.where((slot >= 0) & (slot < prior_keys.shape[0]), slot, found)

    slot = lax.fori_loop(0, table.shape[0], look, 0)
    pages = [
        pltpu.make_async_copy(prior_keys.at[slot], prior.at[:, :128], sems.at[8]),
        pltpu.make_async_copy(prior_values.at[slot], prior.at[:, 128:], sems.at[9]),
    ]
    for copy in pages:
        copy.start()
    for copy in copies[1:4]:
        copy.wait()
    row = lax.broadcasted_iota(jnp.int32, (BLOCK, 128), 0)
    lane = lanes_of((BLOCK, 128))
    for b in range(blocks):
        base = prior_len + order_s[me * blocks + b] * BLOCK
        angle = (base + row).astype(F32) * freq_v[...]
        part = pl.ds(b * BLOCK, BLOCK)
        sine = jnp.sin(angle)
        cos_out[part, :] = jnp.cos(angle)
        sin_out[part, :] = jnp.where(lane % 64 < 32, -sine, sine)
    for copy in copies[4:6]:
        copy.wait()
    wide = hidden_v[...].astype(F32)
    mean = jnp.mean(wide * wide, axis=-1, keepdims=True)
    normed = (wide * lax.rsqrt(mean + EPS) * gain_v[...]).astype(BF16)
    normed_out[...] = normed
    for copy in copies[6:]:
        copy.wait()
    keys = jnp.dot(normed, w_key_v[...], preferred_element_type=F32)
    values = jnp.dot(normed, w_value_v[...], preferred_element_type=F32)
    rotated = norm_and_rotate(keys, twice(key_gain_v), cos_out[...], sin_out[...])
    kv[:, :128] = rotated.astype(BF16)
    kv[:, 128:] = values.astype(BF16)
    for copy in pages + later:
        copy.wait()


def half_rows(ref, core):
    return pl.ds(pl.multiple_of(core * ref.shape[0], ref.shape[0]), ref.shape[0])


def columns(ref, other):
    x = lax.axis_index("head")
    x = 1 - x if other else x
    return pl.ds(pl.multiple_of(x * ref.shape[1], ref.shape[1]), ref.shape[1])


def query_kernel(
    normed, w_query, cosine, sine, query_gain, order, live, masks,
    q_out, own_bias, span_bias, query_gain_v, order_s, live_s, masks_s, sems,
):
    pairs = [
        (order, order_s), (live, live_s), (masks, masks_s), (query_gain, query_gain_v)
    ]
    copies = [pltpu.make_async_copy(a, b, sems.at[i]) for i, (a, b) in enumerate(pairs)]
    for copy in copies:
        copy.start()
    rows = normed.shape[0]
    blocks = rows // BLOCK
    tiles = w_query.shape[1] // 128
    per_kv = tiles // 2
    group = 2 * per_kv
    queries = jnp.dot(normed[...], w_query[...], preferred_element_type=F32)
    for copy in copies:
        copy.wait()
    gain = twice(query_gain_v)
    left = lanes_of((rows, 128)) < 64
    for t in range(tiles):
        kv_head, u = divmod(t, per_kv)
        x = norm_and_rotate(queries[:, t * 128 : (t + 1) * 128], gain, cosine[...], sine[...])
        x = x * (64**-0.5 * LOG2E)
        turned = pltpu.roll(x, 64, 1)
        pair = (x, turned) if kv_head == 0 else (turned, x)
        for odd, head in enumerate(pair):
            kept = jnp.where(left if kv_head == 0 else ~left, head, 0.0)
            high = kept.astype(BF16)
            low = (kept - high.astype(F32)).astype(BF16)
            both = jnp.concatenate([high, low], axis=-1)
            for b in range(blocks):
                at = ((kv_head * blocks + b) * group + 2 * u + odd) * BLOCK
                q_out[at : at + BLOCK, :] = both[b * BLOCK : (b + 1) * BLOCK, :]

    me = lax.axis_index("seq")
    logical = [order_s[me * blocks + b] for b in range(blocks)]
    key_at = lanes_of((BLOCK, blocks * BLOCK))
    row = lax.broadcasted_iota(jnp.int32, key_at.shape, 0)
    for b in range(blocks):
        bias = jnp.full(key_at.shape, MASKED, F32)
        for kb in range(blocks):
            alive = live_s[logical[kb]] > 0
            here = key_at // BLOCK == kb
            if kb == b:
                here = here & (key_at % BLOCK <= row)
            else:
                alive = alive & (logical[kb] < logical[b])
            bias = jnp.where(here, jnp.where(alive, 0.0, MASKED), bias)
        own_bias[b * BLOCK : (b + 1) * BLOCK, :] = bias

    count = masks.shape[0]
    lane = lanes_of((1, PAGE))

    def visit(i, carry):
        rank = me ^ masks_s[i]
        held = [order_s[rank * 2 + half] for half in range(2)]
        alive = [(live_s[block] > 0) & (rank != me) for block in held]
        for b in range(blocks):
            value = [
                jnp.where(alive[h] & (held[h] < logical[b]), 0.0, MASKED) for h in range(2)
            ]
            at = pl.ds(pl.multiple_of(i * PAGE, PAGE), PAGE)
            span_bias[b : b + 1, at] = jnp.where(lane < BLOCK, value[0], value[1])
        return carry

    lax.fori_loop(0, count, visit, 0)


class Piece:
    def __init__(self, rows, biases):
        keys, values = rows[:, :128], rows[:, 128:]
        left = lanes_of(values.shape) < 64
        ones = jnp.ones_like(values)
        self.keys = jnp.concatenate([keys, keys], axis=-1)
        self.values = [jnp.where(left, values, ones), jnp.where(left, ones, values)]
        self.biases = biases


def fold(q, m_in, acc_in, m_out, acc_out, pieces, blocks, part):
    tiles = 2 * blocks
    scores, weights = {}, {}

    def score(t):
        rows = pl.ds(t * part, part)
        scores[t] = []
        for piece in pieces:
            s = lax.dot_general(
                q[rows, :], piece.keys, (((1,), (1,)), ((), ())), preferred_element_type=F32
            )
            scores[t].append(s if piece.biases is None else s + piece.biases[t % blocks])

    def weigh(t):
        rows = pl.ds(t * part, part)
        top = functools.reduce(jnp.maximum, [jnp.max(s, -1, keepdims=True) for s in scores[t]])
        factor = None
        if m_in is not None:
            old = m_in[rows, :1]
            top = jnp.maximum(top, old)
            factor = jnp.exp2(old - top)
        if m_out is not None:
            m_out[rows, :] = jnp.broadcast_to(top, (part, 128))
        weights[t] = [jnp.exp2(s - top).astype(BF16) for s in scores[t]], factor
        del scores[t]

    def mix(t):
        rows = pl.ds(t * part, part)
        parts, factor = weights.pop(t)
        total = 0.0 if factor is None else acc_in[rows, :] * factor
        for p, piece in zip(parts, pieces):
            total = total + jnp.dot(p, piece.values[t // blocks], preferred_element_type=F32)
        acc_out[rows, :] = total

    score(0)
    for t in range(tiles + 1):
        if t + 1 < tiles:
            score(t + 1)
        if t < tiles:
            weigh(t)
        if t > 0:
            mix(t - 1)


def attention_kernel(n_chunks, own, first, last, step, blocks, group, *refs):
    refs = list(refs)
    q = refs.pop(0)
    own_kv, own_bias = (refs.pop(0), refs.pop(0)) if own else (None, None)
    chunks = [refs.pop(0) for _ in range(n_chunks)]
    bias = None if own else refs.pop(0)
    m_in, acc_in = (None, None) if first else (refs.pop(0), refs.pop(0))
    out = refs.pop(0) if last else None
    m_ref, acc_ref = refs.pop(0), refs.pop(0)
    part = group * BLOCK

    def piece(rows, at):
        if bias is None:
            return Piece(rows, None)
        size = rows.shape[0]
        return Piece(rows, [bias[b : b + 1, pl.ds(at, size)] for b in range(blocks)])

    extra = []
    if own:
        mine = [own_bias[b * BLOCK : (b + 1) * BLOCK, :] for b in range(blocks)]
        extra = [Piece(own_kv[...], [jnp.concatenate([m] * group, axis=0) for m in mine])]
    if not refs:
        pieces, at = [], 0
        for chunk in chunks:
            pieces.append(piece(chunk[...], at))
            at += chunk.shape[0]
        fold(q, m_in, acc_in, m_ref, acc_ref, pieces + extra, blocks, part)
    else:
        held, sems = refs
        copies, at = [], 0
        for i, chunk in enumerate(chunks):
            size = chunk.shape[0]
            copies.append(pltpu.make_async_copy(chunk, held.at[pl.ds(at, size)], sems.at[i]))
            at += size
        for copy in copies:
            copy.start()
        for copy in copies:
            copy.wait()

        def visit(c, m_from, acc_from, more):
            first_row = pl.multiple_of(c * step, step)
            pieces = [piece(held[pl.ds(first_row, step), :], first_row)]
            fold(q, m_from, acc_from, m_ref, acc_ref, pieces + more, blocks, part)

        visit(0, m_in, acc_in, extra)
        pl.loop(1, at // step)(lambda c: visit(c, m_ref, acc_ref, []))

    if last:
        left = lanes_of((BLOCK, 128)) < 64
        for kv_head in range(2):
            for b in range(blocks):
                for u in range(group // 2):
                    heads = []
                    for odd in range(2):
                        at = ((kv_head * blocks + b) * group + 2 * u + odd) * BLOCK
                        acc = acc_ref[at : at + BLOCK, :]
                        ratio = acc / pltpu.roll(acc, 64, 1)
                        heads.append(pltpu.roll(ratio, 64, 1) if odd != kv_head else ratio)
                    both = jnp.where(left, heads[0], heads[1]).astype(BF16)
                    tile = kv_head * (group // 2) + u
                    out[b * BLOCK : (b + 1) * BLOCK, tile * 128 : (tile + 1) * 128] = both


def attention(q, own, chunks, bias, state, last, blocks, group):
    rows = sum(c.shape[0] for c in chunks)
    step = min(1024, rows)
    direct = rows <= 2048
    first = state is None
    operands = [q, *(own or ()), *chunks, *([] if bias is None else [bias]), *(state or ())]
    specs = [spec(VMEM)] * len(operands)
    if not direct:
        at = 1 + len(own or ())
        specs[at : at + len(chunks)] = [spec(pl.ANY)] * len(chunks)
    n = q.shape[0]
    pair = [jax.ShapeDtypeStruct((n, 128), F32)] * 2
    scratch = []
    if not direct:
        scratch = [VMEM((rows, 256), BF16), pltpu.SemaphoreType.DMA((len(chunks),))]
    if last:
        outs = jax.ShapeDtypeStruct((blocks * BLOCK, 2 * group * 64), BF16)
        out_specs = spec(VMEM)
        scratch = [VMEM((n, 128), F32)] * 2 + scratch
    else:
        outs, out_specs = pair, [spec(VMEM)] * 2
    return pl.pallas_call(
        functools.partial(
            attention_kernel, len(chunks), own is not None, first, last, step, blocks, group
        ),
        out_shape=outs,
        in_specs=specs,
        out_specs=out_specs,
        scratch_shapes=scratch,
        compiler_params=params(32),
        cost_estimate=cost(4 * n * rows * 256, rows * 512 + n * 2048),
    )(*operands)


def pages_kernel(n_chunks, dest, order, where, mine, w_output, *refs):
    chunks, (keys, values, partial, w_mine, sems) = refs[:n_chunks], refs[n_chunks:]
    me = lax.axis_index("seq")
    copy = pltpu.make_async_copy(w_output.at[:, columns(w_mine, 0)], w_mine, sems.at[2])
    copy.start()

    def find(table):
        def body(wanted):
            return lax.fori_loop(
                0, table.shape[0], lambda i, f: jnp.where(table[i] == wanted, i, f), 0
            )

        return body

    page = find(dest)(me)
    for half in range(2):
        source = find(order)(page * 2 + half)
        slot = where[me ^ (source // 2)]
        row = slot * PAGE + (source % 2) * BLOCK
        at = 0
        for chunk in chunks:
            size = chunk.shape[0]
            inside = (row >= at) & (row < at + size)

            @pl.when(inside)
            def _(chunk=chunk, at=at):
                rows = pl.ds(pl.multiple_of(row - at, BLOCK), BLOCK)
                to = pl.ds(half * BLOCK, BLOCK)
                a = pltpu.make_async_copy(chunk.at[rows, :128], keys.at[0, to], sems.at[0])
                b = pltpu.make_async_copy(chunk.at[rows, 128:], values.at[0, to], sems.at[1])
                a.start()
                b.start()
                a.wait()
                b.wait()

            at += size
    copy.wait()
    partial[...] = jnp.dot(mine[...], w_mine[...], preferred_element_type=F32)


def project_kernel(partial, peer, w_near, w_far, out):
    even = lax.axis_index("seq") % 2 == 0
    depth = w_near.shape[0]
    low, high = peer[:, :depth], peer[:, depth:]
    near = jnp.where(even, low, high)
    far = jnp.where(even, high, low)
    total = partial[...] + jnp.dot(near, w_near[...], preferred_element_type=F32)
    out[...] = total + jnp.dot(far, w_far[...], preferred_element_type=F32)


def plan(n):
    bits = [1 << i for i in range(n.bit_length() - 2, 0, -1)]
    return bits, bits[-1:] + bits[:-1]


def slot_masks(steps):
    masks = [0]
    for step in steps + [1]:
        masks = masks + [m ^ step for m in masks]
    return np.array(masks, np.int32)


def swap(x, n, step):
    return lax.ppermute(x, "seq", [(i, i ^ step) for i in range(n)])


def grow(held, n, step):
    return jnp.concatenate([held, swap(held, n, step)], axis=0)


def after(x, *others):
    return lax.optimization_barrier((x, *others))[0]


def body(
    n,
    hidden_in,
    attn_gain,
    w_query,
    w_key,
    w_value,
    query_gain,
    key_gain,
    w_output,
    prior_keys,
    prior_values,
    span_order,
    key_live,
    page_table,
    page_dest,
):
    rows, width = hidden_in.shape
    blocks = rows // BLOCK
    head_dim = query_gain.shape[0]
    group = w_query.shape[1] // w_key.shape[1]
    prior_len = page_table.shape[0] * PAGE
    out_width = w_output.shape[1] // 2
    depth = w_output.shape[0] // 2
    steps, span_steps = plan(n)
    masks = slot_masks(span_steps)
    where = np.zeros_like(masks)
    where[masks] = np.arange(n)
    half = head_dim // 2
    freq = np.tile((10000.0 ** (-np.arange(half) / half)).astype(np.float32), 4)[None, :]

    kv, prior, normed, cosine, sine, w_query, w_send = pl.pallas_call(
        functools.partial(kv_kernel, prior_len),
        out_shape=[
            jax.ShapeDtypeStruct((rows, 256), BF16),
            jax.ShapeDtypeStruct((PAGE, 256), BF16),
            jax.ShapeDtypeStruct((rows, width), BF16),
            jax.ShapeDtypeStruct((rows, 128), F32),
            jax.ShapeDtypeStruct((rows, 128), F32),
            jax.ShapeDtypeStruct(w_query.shape, BF16),
            jax.ShapeDtypeStruct((depth, out_width), BF16),
        ],
        in_specs=[spec(pltpu.HBM)] * 12,
        out_specs=[spec(VMEM)] * 7,
        scratch_shapes=[
            SMEM(span_order.shape, jnp.int32),
            SMEM(page_table.shape, jnp.int32),
            VMEM(hidden_in.shape, BF16),
            VMEM((1, width), F32),
            VMEM(w_key.shape, BF16),
            VMEM(w_value.shape, BF16),
            VMEM((1, head_dim), F32),
            VMEM((1, 128), F32),
            pltpu.SemaphoreType.DMA((12,)),
        ],
        compiler_params=params(),
        cost_estimate=cost(2 * rows * width * 256, 3 << 20),
    )(
        *in_hbm(
            span_order,
            page_table,
            hidden_in,
            attn_gain.reshape(1, -1),
            w_key,
            w_value,
            key_gain.reshape(1, -1),
            jnp.asarray(freq),
            prior_keys,
            prior_values,
            w_query,
            w_output,
        )
    )

    with jax.named_scope("prior_step_0"):
        prior = grow(prior, n, steps[0])
    with jax.named_scope("span_step_0"):
        span = grow(kv, n, span_steps[0])
    normed = after(normed, prior, span)
    with jax.named_scope("weights_step"):
        w_near = lax.ppermute(w_send, "head", [(0, 1), (1, 0)])
        w_far = swap(w_near, n, 1)
    q, own_bias, span_bias = pl.pallas_call(
        query_kernel,
        out_shape=[
            jax.ShapeDtypeStruct((2 * blocks * group * BLOCK, 256), BF16),
            jax.ShapeDtypeStruct((rows, rows), F32),
            jax.ShapeDtypeStruct((blocks, n * PAGE), F32),
        ],
        in_specs=[spec(VMEM)] * 4 + [spec(pltpu.HBM)] * 4,
        out_specs=[spec(VMEM)] * 3,
        scratch_shapes=[
            VMEM((1, head_dim), F32),
            SMEM(span_order.shape, jnp.int32),
            SMEM(key_live.shape, jnp.int32),
            SMEM((masks.size,), jnp.int32),
            pltpu.SemaphoreType.DMA((4,)),
        ],
        compiler_params=params(),
        cost_estimate=cost(2 * rows * width * 512, 4 << 20),
    )(
        normed,
        w_query,
        cosine,
        sine,
        *in_hbm(query_gain.reshape(1, -1), span_order, key_live, jnp.asarray(masks.reshape(-1))),
    )

    for i, step in enumerate(steps[1:-1], 1):
        with jax.named_scope(f"prior_step_{i}"):
            prior = grow(prior, n, step)
        with jax.named_scope(f"span_step_{i}"):
            span = grow(span, n, span_steps[i])
    prior, span, _ = lax.optimization_barrier((prior, span, q))
    with jax.named_scope("prior_last"):
        prior_same = [prior, swap(prior, n, steps[-1])]
    with jax.named_scope("span_last"):
        span_same = [span, swap(span, n, span_steps[-1])]
    with jax.named_scope("prior_core"):
        prior_other = [swap(c, n, 1) for c in prior_same]
    with jax.named_scope("span_core"):
        span_other = [swap(c, n, 1) for c in span_same]

    common = dict(blocks=blocks, group=group)
    edge = n // 2 * PAGE
    state = attention(q, (kv, own_bias), prior_same + prior_other, None, None, False, **common)
    state = attention(q, None, span_same, span_bias[:, :edge], state, False, **common)
    heads = attention(q, None, span_other, span_bias[:, edge:], state, True, **common)
    peer = lax.ppermute(heads, "head", [(0, 1), (1, 0)])

    all_span = span_same + span_other
    new_keys, new_values, partial = pl.pallas_call(
        functools.partial(pages_kernel, len(all_span)),
        out_shape=[jax.ShapeDtypeStruct((1, PAGE, 128), BF16)] * 2
        + [jax.ShapeDtypeStruct((rows, out_width), F32)],
        in_specs=[spec(SMEM)] * 3 + [spec(VMEM), spec(pltpu.HBM)] + [spec(pl.ANY)] * len(all_span),
        out_specs=[spec(VMEM)] * 3,
        scratch_shapes=[
            VMEM((w_output.shape[0], out_width), BF16),
            pltpu.SemaphoreType.DMA((3,)),
        ],
        compiler_params=params(),
        cost_estimate=cost(2 * rows * 512 * out_width, 1 << 21),
    )(page_dest, span_order, jnp.asarray(where), heads, *in_hbm(w_output), *all_span)

    attn_out = pl.pallas_call(
        project_kernel,
        out_shape=jax.ShapeDtypeStruct((rows, out_width), F32),
        in_specs=[spec(VMEM)] * 4,
        out_specs=spec(VMEM),
        compiler_params=params(),
        cost_estimate=cost(2 * rows * 512 * out_width, 2 << 20),
    )(partial, peer, w_near, w_far)
    return attn_out, new_keys, new_values


def solution(mesh):
    return jax.shard_map(
        functools.partial(body, mesh.shape["seq"]),
        mesh=mesh,
        in_specs=(
            P("seq", None),
            P(),
            P(None, "head"),
            P(None, "head"),
            P(None, "head"),
            P(),
            P(),
            P("head", None),
            P("seq", None, "head"),
            P("seq", None, "head"),
            P(),
            P(),
            P(),
            P(),
        ),
        out_specs=(P("seq", "head"), P("seq", None, "head"), P("seq", None, "head")),
        check_vma=False,
    )
```

```python
import functools

import jax
import jax.numpy as jnp
import numpy as np
from jax import lax
from jax.experimental import pallas as pl
from jax.experimental.pallas import tpu as pltpu
from jax.sharding import PartitionSpec as P

PAGE = 128
BLOCK = 64
EPS = 1e-06
MASKED = -1e30
F32 = jnp.float32
BF16 = jnp.bfloat16
VMEM = pltpu.VMEM
SMEM = pltpu.SMEM
LOG2E = 1.4426950408889634


def spec(space):
    return pl.BlockSpec(memory_space=space)


def in_hbm(*arrays):
    return [pltpu.with_memory_space_constraint(a, pltpu.HBM) for a in arrays]


def params(mib=32):
    return pltpu.CompilerParams(vmem_limit_bytes=mib * 1024 * 1024)


def cost(flops, size):
    return pl.CostEstimate(flops=int(flops), bytes_accessed=int(size), transcendentals=0)


def lanes_of(shape):
    return lax.broadcasted_iota(jnp.int32, shape, len(shape) - 1)


def norm_and_rotate(x, gain, cosine, sine):
    lane = lanes_of(x.shape)
    left = lane < 64
    square = x * x
    sum_left = jnp.sum(jnp.where(left, square, 0.0), axis=-1, keepdims=True)
    sum_right = jnp.sum(jnp.where(left, 0.0, square), axis=-1, keepdims=True)
    mean = jnp.where(left, sum_left, sum_right) * (1.0 / 64)
    y = x * lax.rsqrt(mean + EPS) * gain
    swapped = jnp.where(lane % 64 < 32, pltpu.roll(y, 96, 1), pltpu.roll(y, 32, 1))
    return y * cosine + swapped * sine


def twice(gain_ref):
    gain = gain_ref[...]
    return jnp.concatenate([gain, gain], axis=-1)


def kv_kernel(
    prior_len, order, table, hidden, gain, w_key, w_value, key_gain, freq, prior_keys, prior_values,
    w_output,
    kv, prior, normed_out, cos_out, sin_out, w_send,
    order_s, table_s, hidden_v, gain_v, w_key_v, w_value_v, key_gain_v, freq_v, sems,
):
    rows = hidden.shape[0]
    blocks = rows // BLOCK
    me = lax.axis_index("seq")
    pairs = [
        (table, table_s), (order, order_s), (freq, freq_v), (key_gain, key_gain_v),
        (gain, gain_v), (hidden, hidden_v), (w_key, w_key_v), (w_value, w_value_v),
    ]
    copies = [pltpu.make_async_copy(a, b, sems.at[i]) for i, (a, b) in enumerate(pairs)]
    later = [
        pltpu.make_async_copy(
            w_output.at[half_rows(w_send, me % 2), columns(w_send, 1)], w_send, sems.at[10]
        ),
    ]
    for copy in copies + later:
        copy.start()
    copies[0].wait()
    first = me * prior_keys.shape[0]

    def look(i, found):
        slot = table_s[i] - first
        return jnp.where((slot >= 0) & (slot < prior_keys.shape[0]), slot, found)

    slot = lax.fori_loop(0, table.shape[0], look, 0)
    pages = [
        pltpu.make_async_copy(prior_keys.at[slot], prior.at[:, :128], sems.at[8]),
        pltpu.make_async_copy(prior_values.at[slot], prior.at[:, 128:], sems.at[9]),
    ]
    for copy in pages:
        copy.start()
    for copy in copies[1:4]:
        copy.wait()
    row = lax.broadcasted_iota(jnp.int32, (BLOCK, 128), 0)
    lane = lanes_of((BLOCK, 128))
    for b in range(blocks):
        base = prior_len + order_s[me * blocks + b] * BLOCK
        angle = (base + row).astype(F32) * freq_v[...]
        part = pl.ds(b * BLOCK, BLOCK)
        sine = jnp.sin(angle)
        cos_out[part, :] = jnp.cos(angle)
        sin_out[part, :] = jnp.where(lane % 64 < 32, -sine, sine)
    for copy in copies[4:6]:
        copy.wait()
    wide = hidden_v[...].astype(F32)
    mean = jnp.mean(wide * wide, axis=-1, keepdims=True)
    normed = (wide * lax.rsqrt(mean + EPS) * gain_v[...]).astype(BF16)
    normed_out[...] = normed
    for copy in copies[6:]:
        copy.wait()
    keys = jnp.dot(normed, w_key_v[...], preferred_element_type=F32)
    values = jnp.dot(normed, w_value_v[...], preferred_element_type=F32)
    rotated = norm_and_rotate(keys, twice(key_gain_v), cos_out[...], sin_out[...])
    kv[:, :128] = rotated.astype(BF16)
    kv[:, 128:] = values.astype(BF16)
    for copy in pages + later:
        copy.wait()


def half_rows(ref, core):
    return pl.ds(pl.multiple_of(core * ref.shape[0], ref.shape[0]), ref.shape[0])


def columns(ref, other):
    x = lax.axis_index("head")
    x = 1 - x if other else x
    return pl.ds(pl.multiple_of(x * ref.shape[1], ref.shape[1]), ref.shape[1])


def query_kernel(
    normed, cosine, sine, w_query, query_gain, q_out, w_query_v, query_gain_v, sems
):
    pairs = [(w_query, w_query_v), (query_gain, query_gain_v)]
    copies = [pltpu.make_async_copy(a, b, sems.at[i]) for i, (a, b) in enumerate(pairs)]
    for copy in copies:
        copy.start()
    rows = normed.shape[0]
    blocks = rows // BLOCK
    tiles = w_query.shape[1] // 128
    per_kv = tiles // 2
    group = 2 * per_kv
    for copy in copies:
        copy.wait()
    queries = jnp.dot(normed[...], w_query_v[...], preferred_element_type=F32)
    gain = twice(query_gain_v)
    left = lanes_of((rows, 128)) < 64
    for t in range(tiles):
        kv_head, u = divmod(t, per_kv)
        x = norm_and_rotate(queries[:, t * 128 : (t + 1) * 128], gain, cosine[...], sine[...])
        x = x * (64**-0.5 * LOG2E)
        turned = pltpu.roll(x, 64, 1)
        pair = (x, turned) if kv_head == 0 else (turned, x)
        for odd, head in enumerate(pair):
            kept = jnp.where(left if kv_head == 0 else ~left, head, 0.0)
            high = kept.astype(BF16)
            low = (kept - high.astype(F32)).astype(BF16)
            both = jnp.concatenate([high, low], axis=-1)
            for b in range(blocks):
                at = ((kv_head * blocks + b) * group + 2 * u + odd) * BLOCK
                q_out[at : at + BLOCK, :] = both[b * BLOCK : (b + 1) * BLOCK, :]


def mask_kernel(blocks, order, live, masks, turn, own_bias, span_bias, order_s, live_s, masks_s, sems):
    pairs = [(order, order_s), (live, live_s), (masks, masks_s)]
    copies = [pltpu.make_async_copy(a, b, sems.at[i]) for i, (a, b) in enumerate(pairs)]
    for copy in copies:
        copy.start()
    for copy in copies:
        copy.wait()
    me = lax.axis_index("seq")
    logical = [order_s[me * blocks + b] for b in range(blocks)]
    key_at = lanes_of((BLOCK, blocks * BLOCK))
    row = lax.broadcasted_iota(jnp.int32, key_at.shape, 0)
    for b in range(blocks):
        bias = jnp.full(key_at.shape, MASKED, F32)
        for kb in range(blocks):
            alive = live_s[logical[kb]] > 0
            here = key_at // BLOCK == kb
            if kb == b:
                here = here & (key_at % BLOCK <= row)
            else:
                alive = alive & (logical[kb] < logical[b])
            bias = jnp.where(here, jnp.where(alive, 0.0, MASKED), bias)
        own_bias[b * BLOCK : (b + 1) * BLOCK, :] = bias

    count = masks.shape[0]
    lane = lanes_of((1, PAGE))

    def visit(i, carry):
        rank = me ^ masks_s[i]
        held = [order_s[rank * 2 + half] for half in range(2)]
        alive = [(live_s[block] > 0) & (rank != me) for block in held]
        for b in range(blocks):
            value = [
                jnp.where(alive[h] & (held[h] < logical[b]), 0.0, MASKED) for h in range(2)
            ]
            at = pl.ds(pl.multiple_of(i * PAGE, PAGE), PAGE)
            span_bias[b : b + 1, at] = jnp.where(lane < BLOCK, value[0], value[1])
        return carry

    lax.fori_loop(0, count, visit, 0)


class Piece:
    def __init__(self, rows, biases):
        keys, values = rows[:, :128], rows[:, 128:]
        left = lanes_of(values.shape) < 64
        ones = jnp.ones_like(values)
        self.keys = jnp.concatenate([keys, keys], axis=-1)
        self.values = [jnp.where(left, values, ones), jnp.where(left, ones, values)]
        self.biases = biases


def fold(q, m_in, acc_in, m_out, acc_out, pieces, blocks, part, finish=None):
    tiles = 2 * blocks
    scores, weights = {}, {}

    def score(t):
        rows = pl.ds(t * part, part)
        scores[t] = []
        for piece in pieces:
            s = lax.dot_general(
                q[rows, :], piece.keys, (((1,), (1,)), ((), ())), preferred_element_type=F32
            )
            scores[t].append(s if piece.biases is None else s + piece.biases[t % blocks])

    def weigh(t):
        rows = pl.ds(t * part, part)
        top = functools.reduce(jnp.maximum, [jnp.max(s, -1, keepdims=True) for s in scores[t]])
        factor = None
        if m_in is not None:
            old = m_in[rows, :1]
            top = jnp.maximum(top, old)
            factor = jnp.exp2(old - top)
        if finish is None:
            m_out[rows, :] = jnp.broadcast_to(top, (part, 128))
        weights[t] = [jnp.exp2(s - top).astype(BF16) for s in scores[t]], factor
        del scores[t]

    def mix(t):
        rows = pl.ds(t * part, part)
        parts, factor = weights.pop(t)
        total = 0.0 if factor is None else acc_in[rows, :] * factor
        for p, piece in zip(parts, pieces):
            total = total + jnp.dot(p, piece.values[t // blocks], preferred_element_type=F32)
        if finish is None:
            acc_out[rows, :] = total
        else:
            finish(t, total)

    score(0)
    for t in range(tiles + 1):
        if t + 1 < tiles:
            score(t + 1)
        if t < tiles:
            weigh(t)
        if t > 0:
            mix(t - 1)


def attention_kernel(offsets, own, first, last, step, blocks, group, *refs):
    refs = list(refs)
    q = refs.pop(0)
    own_kv, own_bias = (refs.pop(0), refs.pop(0)) if own else (None, None)
    chunks = [refs.pop(0) for _ in offsets]
    bias = refs.pop(0)
    m_in, acc_in = (None, None) if first else (refs.pop(0), refs.pop(0))
    out = refs.pop(0) if last else None
    m_ref, acc_ref = refs.pop(0), refs.pop(0)
    part = group * BLOCK

    def piece(rows, at):
        if at is None:
            return Piece(rows, None)
        size = rows.shape[0]
        return Piece(rows, [bias[b : b + 1, pl.ds(at, size)] for b in range(blocks)])

    extra = []
    if own:
        mine = [own_bias[b * BLOCK : (b + 1) * BLOCK, :] for b in range(blocks)]
        extra = [Piece(own_kv[...], [jnp.concatenate([m] * group, axis=0) for m in mine])]

    def finish(t, acc):
        kv_head, b = divmod(t, blocks)
        left = lanes_of((BLOCK, 128)) < 64
        for u in range(group // 2):
            even = acc[2 * u * BLOCK : (2 * u + 1) * BLOCK, :]
            odd = acc[(2 * u + 1) * BLOCK : (2 * u + 2) * BLOCK, :]
            even_t, odd_t = pltpu.roll(even, 64, 1), pltpu.roll(odd, 64, 1)
            if kv_head == 0:
                top, low = jnp.where(left, even, odd_t), jnp.where(left, even_t, odd)
            else:
                top, low = jnp.where(left, even_t, odd), jnp.where(left, even, odd_t)
            tile = kv_head * (group // 2) + u
            rows = slice(b * BLOCK, (b + 1) * BLOCK)
            out[rows, tile * 128 : (tile + 1) * 128] = (top / low).astype(BF16)

    if not refs:
        pieces = [piece(chunk[...], at) for chunk, at in zip(chunks, offsets)]
        fold(
            q, m_in, acc_in, m_ref, acc_ref, pieces + extra, blocks, part, finish if last else None
        )
        return
    held, sem = refs
    if own:
        fold(q, m_in, acc_in, m_ref, acc_ref, extra, blocks, part)
    elif not first:
        m_ref[...] = m_in[...]
        acc_ref[...] = acc_in[...]
    for chunk, at in zip(chunks, offsets):

        def visit(c, chunk=chunk, at=at):
            first_row = pl.multiple_of(c * step, step)
            copy = pltpu.make_async_copy(chunk.at[pl.ds(first_row, step)], held, sem)
            copy.start()
            copy.wait()
            pieces = [piece(held[...], None if at is None else at + first_row)]
            fold(q, m_ref, acc_ref, m_ref, acc_ref, pieces, blocks, part)

        pl.loop(0, chunk.shape[0] // step)(visit)
    if last:
        for t in range(2 * blocks):
            finish(t, acc_ref[t * part : (t + 1) * part, :])


def attention(q, own, chunks, bias, state, last, blocks, group):
    arrays, offsets = zip(*chunks)
    rows = sum(c.shape[0] for c in arrays)
    direct = rows <= 2048
    step = min(1024, *(c.shape[0] for c in arrays))
    first = state is None
    operands = [q, *(own or ()), *arrays, bias, *(state or ())]
    specs = [spec(VMEM)] * len(operands)
    if not direct:
        at = 1 + len(own or ())
        specs[at : at + len(arrays)] = [spec(pl.ANY)] * len(arrays)
    n = q.shape[0]
    pair = [jax.ShapeDtypeStruct((n, 128), F32)] * 2
    scratch = []
    if not direct:
        scratch = [VMEM((step, 256), BF16), pltpu.SemaphoreType.DMA]
    if last:
        outs = jax.ShapeDtypeStruct((blocks * BLOCK, 2 * group * 64), BF16)
        out_specs = spec(VMEM)
        scratch = [VMEM((n, 128), F32)] * 2 + scratch
    else:
        outs, out_specs = pair, [spec(VMEM)] * 2
    return pl.pallas_call(
        functools.partial(
            attention_kernel, offsets, own is not None, first, last, step, blocks, group
        ),
        out_shape=outs,
        in_specs=specs,
        out_specs=out_specs,
        scratch_shapes=scratch,
        compiler_params=params(32),
        cost_estimate=cost(4 * n * rows * 256, rows * 512 + n * 2048),
    )(*operands)


def pages_kernel(n_chunks, dest, order, where, mine, w_output, *refs):
    chunks, (keys, values, partial, w_mine, sems) = refs[:n_chunks], refs[n_chunks:]
    me = lax.axis_index("seq")
    copy = pltpu.make_async_copy(w_output.at[:, columns(w_mine, 0)], w_mine, sems.at[2])
    copy.start()

    def find(table):
        def body(wanted):
            return lax.fori_loop(
                0, table.shape[0], lambda i, f: jnp.where(table[i] == wanted, i, f), 0
            )

        return body

    page = find(dest)(me)
    for half in range(2):
        source = find(order)(page * 2 + half)
        slot = where[me ^ (source // 2)]
        row = slot * PAGE + (source % 2) * BLOCK
        at = 0
        for chunk in chunks:
            size = chunk.shape[0]
            inside = (row >= at) & (row < at + size)

            @pl.when(inside)
            def _(chunk=chunk, at=at):
                rows = pl.ds(pl.multiple_of(row - at, BLOCK), BLOCK)
                to = pl.ds(half * BLOCK, BLOCK)
                a = pltpu.make_async_copy(chunk.at[rows, :128], keys.at[0, to], sems.at[0])
                b = pltpu.make_async_copy(chunk.at[rows, 128:], values.at[0, to], sems.at[1])
                a.start()
                b.start()
                a.wait()
                b.wait()

            at += size
    copy.wait()
    partial[...] = jnp.dot(mine[...], w_mine[...], preferred_element_type=F32)


def project_kernel(partial, peer, w_near, w_far, out):
    even = lax.axis_index("seq") % 2 == 0
    depth = w_near.shape[0]
    low, high = peer[:, :depth], peer[:, depth:]
    near = jnp.where(even, low, high)
    far = jnp.where(even, high, low)
    total = partial[...] + jnp.dot(near, w_near[...], preferred_element_type=F32)
    out[...] = total + jnp.dot(far, w_far[...], preferred_element_type=F32)


def plan(n):
    bits = [1 << i for i in range(n.bit_length() - 2, 0, -1)]
    return bits, bits[-1:] + bits[:-1]


def slot_masks(steps):
    masks = [0]
    for step in steps + [1]:
        masks = masks + [m ^ step for m in masks]
    return np.array(masks, np.int32)


def swap(x, n, step):
    return lax.ppermute(x, "seq", [(i, i ^ step) for i in range(n)])


def grow(held, n, step):
    return jnp.concatenate([held, swap(held, n, step)], axis=0)


def after(x, *others):
    return lax.optimization_barrier((x, *others))[0]


def body(
    n,
    hidden_in,
    attn_gain,
    w_query,
    w_key,
    w_value,
    query_gain,
    key_gain,
    w_output,
    prior_keys,
    prior_values,
    span_order,
    key_live,
    page_table,
    page_dest,
):
    rows, width = hidden_in.shape
    blocks = rows // BLOCK
    head_dim = query_gain.shape[0]
    group = w_query.shape[1] // w_key.shape[1]
    prior_len = page_table.shape[0] * PAGE
    out_width = w_output.shape[1] // 2
    depth = w_output.shape[0] // 2
    steps, span_steps = plan(n)
    masks = slot_masks(span_steps)
    where = np.zeros_like(masks)
    where[masks] = np.arange(n)
    half = head_dim // 2
    freq = np.tile((10000.0 ** (-np.arange(half) / half)).astype(np.float32), 4)[None, :]

    kv, prior, normed, cosine, sine, w_send = pl.pallas_call(
        functools.partial(kv_kernel, prior_len),
        out_shape=[
            jax.ShapeDtypeStruct((rows, 256), BF16),
            jax.ShapeDtypeStruct((PAGE, 256), BF16),
            jax.ShapeDtypeStruct((rows, width), BF16),
            jax.ShapeDtypeStruct((rows, 128), F32),
            jax.ShapeDtypeStruct((rows, 128), F32),
            jax.ShapeDtypeStruct((depth, out_width), BF16),
        ],
        in_specs=[spec(pltpu.HBM)] * 11,
        out_specs=[spec(VMEM)] * 6,
        scratch_shapes=[
            SMEM(span_order.shape, jnp.int32),
            SMEM(page_table.shape, jnp.int32),
            VMEM(hidden_in.shape, BF16),
            VMEM((1, width), F32),
            VMEM(w_key.shape, BF16),
            VMEM(w_value.shape, BF16),
            VMEM((1, head_dim), F32),
            VMEM((1, 128), F32),
            pltpu.SemaphoreType.DMA((11,)),
        ],
        compiler_params=params(),
        cost_estimate=cost(2 * rows * width * 256, 3 << 20),
    )(
        *in_hbm(
            span_order,
            page_table,
            hidden_in,
            attn_gain.reshape(1, -1),
            w_key,
            w_value,
            key_gain.reshape(1, -1),
            jnp.asarray(freq),
            prior_keys,
            prior_values,
            w_output,
        )
    )

    with jax.named_scope("prior_step_0"):
        prior = grow(prior, n, steps[0])
    with jax.named_scope("span_step_0"):
        span = grow(kv, n, span_steps[0])
    normed = after(normed, prior, span)
    with jax.named_scope("weights_step"):
        w_near = lax.ppermute(w_send, "head", [(0, 1), (1, 0)])
        w_far = swap(w_near, n, 1)
    q = pl.pallas_call(
        query_kernel,
        out_shape=jax.ShapeDtypeStruct((2 * blocks * group * BLOCK, 256), BF16),
        in_specs=[spec(VMEM)] * 3 + [spec(pltpu.HBM)] * 2,
        out_specs=spec(VMEM),
        scratch_shapes=[
            VMEM(w_query.shape, BF16),
            VMEM((1, head_dim), F32),
            pltpu.SemaphoreType.DMA((2,)),
        ],
        compiler_params=params(),
        cost_estimate=cost(2 * rows * width * 512, 4 << 20),
    )(normed, cosine, sine, *in_hbm(w_query, query_gain.reshape(1, -1)))
    for i, step in enumerate(steps[1:-1], 1):
        with jax.named_scope(f"prior_step_{i}"):
            prior = grow(prior, n, step)
        with jax.named_scope(f"span_step_{i}"):
            span = grow(span, n, span_steps[i])
    prior, span, _ = lax.optimization_barrier((prior, span, q))
    with jax.named_scope("prior_last"):
        prior_far = swap(prior, n, steps[-1])
    with jax.named_scope("span_last"):
        span_far = swap(span, n, span_steps[-1])
    own_bias, span_bias = pl.pallas_call(
        functools.partial(mask_kernel, blocks),
        out_shape=[
            jax.ShapeDtypeStruct((rows, rows), F32),
            jax.ShapeDtypeStruct((blocks, n * PAGE), F32),
        ],
        in_specs=[spec(pltpu.HBM)] * 3 + [spec(pl.ANY)],
        out_specs=[spec(VMEM)] * 2,
        scratch_shapes=[
            SMEM(span_order.shape, jnp.int32),
            SMEM(key_live.shape, jnp.int32),
            SMEM((masks.size,), jnp.int32),
            pltpu.SemaphoreType.DMA((3,)),
        ],
        compiler_params=params(),
        cost_estimate=cost(1 << 28, 1 << 20),
    )(*in_hbm(span_order, key_live, jnp.asarray(masks)), q)
    prior, span = after(prior, own_bias), after(span, own_bias)
    with jax.named_scope("prior_core_near"):
        prior_core = swap(prior, n, 1)
    with jax.named_scope("span_core_near"):
        span_core = swap(span, n, 1)

    common = dict(bias=span_bias, blocks=blocks, group=group)
    part = n // 4 * PAGE
    chunks = [(prior, None), (prior_core, None), (span, 0), (span_core, 2 * part)]
    state = attention(q, (kv, own_bias), chunks, state=None, last=False, **common)
    prior_far, span_far, *state = lax.optimization_barrier((prior_far, span_far, *state))
    with jax.named_scope("prior_core_far"):
        prior_core_far = swap(prior_far, n, 1)
    with jax.named_scope("span_core_far"):
        span_core_far = swap(span_far, n, 1)
    chunks = [(prior_far, None), (span_far, part)]
    state = attention(q, None, chunks, state=state, last=False, **common)
    chunks = [(prior_core_far, None), (span_core_far, 3 * part)]
    heads = attention(q, None, chunks, state=state, last=True, **common)
    peer = lax.ppermute(heads, "head", [(0, 1), (1, 0)])

    all_span = [span, span_far, span_core, span_core_far]
    new_keys, new_values, partial = pl.pallas_call(
        functools.partial(pages_kernel, len(all_span)),
        out_shape=[jax.ShapeDtypeStruct((1, PAGE, 128), BF16)] * 2
        + [jax.ShapeDtypeStruct((rows, out_width), F32)],
        in_specs=[spec(SMEM)] * 3 + [spec(VMEM), spec(pltpu.HBM)] + [spec(pl.ANY)] * len(all_span),
        out_specs=[spec(VMEM)] * 3,
        scratch_shapes=[
            VMEM((w_output.shape[0], out_width), BF16),
            pltpu.SemaphoreType.DMA((3,)),
        ],
        compiler_params=params(),
        cost_estimate=cost(2 * rows * 512 * out_width, 1 << 21),
    )(page_dest, span_order, jnp.asarray(where), heads, *in_hbm(w_output), *all_span)

    attn_out = pl.pallas_call(
        project_kernel,
        out_shape=jax.ShapeDtypeStruct((rows, out_width), F32),
        in_specs=[spec(VMEM)] * 4,
        out_specs=spec(VMEM),
        compiler_params=params(),
        cost_estimate=cost(2 * rows * 512 * out_width, 2 << 20),
    )(partial, peer, w_near, w_far)
    return attn_out, new_keys, new_values


def solution(mesh):
    return jax.shard_map(
        functools.partial(body, mesh.shape["seq"]),
        mesh=mesh,
        in_specs=(
            P("seq", None),
            P(),
            P(None, "head"),
            P(None, "head"),
            P(None, "head"),
            P(),
            P(),
            P("head", None),
            P("seq", None, "head"),
            P("seq", None, "head"),
            P(),
            P(),
            P(),
            P(),
        ),
        out_specs=(P("seq", "head"), P("seq", None, "head"), P("seq", None, "head")),
        check_vma=False,
    )
```

```python
import functools

import jax
import jax.numpy as jnp
import numpy as np
from jax import lax
from jax.experimental import pallas as pl
from jax.experimental.pallas import tpu as pltpu
from jax.sharding import PartitionSpec as P

PAGE = 128
BLOCK = 64
EPS = 1e-06
MASKED = -1e30
F32 = jnp.float32
BF16 = jnp.bfloat16
VMEM = pltpu.VMEM
SMEM = pltpu.SMEM
LOG2E = 1.4426950408889634


def spec(space):
    return pl.BlockSpec(memory_space=space)


def in_hbm(*arrays):
    return [pltpu.with_memory_space_constraint(a, pltpu.HBM) for a in arrays]


def params(mib=32):
    return pltpu.CompilerParams(vmem_limit_bytes=mib * 1024 * 1024)


def cost(flops, size):
    return pl.CostEstimate(flops=int(flops), bytes_accessed=int(size), transcendentals=0)


def lanes_of(shape):
    return lax.broadcasted_iota(jnp.int32, shape, len(shape) - 1)


def norm_and_rotate(x, gain, cosine, sine):
    lane = lanes_of(x.shape)
    left = lane < 64
    square = x * x
    sum_left = jnp.sum(jnp.where(left, square, 0.0), axis=-1, keepdims=True)
    sum_right = jnp.sum(jnp.where(left, 0.0, square), axis=-1, keepdims=True)
    mean = jnp.where(left, sum_left, sum_right) * (1.0 / 64)
    y = x * lax.rsqrt(mean + EPS) * gain
    swapped = jnp.where(lane % 64 < 32, pltpu.roll(y, 96, 1), pltpu.roll(y, 32, 1))
    return y * cosine + swapped * sine


def twice(gain_ref):
    gain = gain_ref[...]
    return jnp.concatenate([gain, gain], axis=-1)


def kv_kernel(
    prior_len, order, table, hidden, gain, w_key, w_value, key_gain, freq, prior_keys, prior_values,
    w_output,
    kv, prior, normed_out, cos_out, sin_out, w_send,
    order_s, table_s, hidden_v, gain_v, w_key_v, w_value_v, key_gain_v, freq_v, sems, late_sems,
):
    rows = hidden.shape[0]
    blocks = rows // BLOCK
    me = lax.axis_index("seq")
    pairs = [
        (table, table_s), (order, order_s), (freq, freq_v), (key_gain, key_gain_v),
        (gain, gain_v), (hidden, hidden_v), (w_key, w_key_v), (w_value, w_value_v),
    ]
    copies = [pltpu.make_async_copy(a, b, sems.at[i]) for i, (a, b) in enumerate(pairs)]
    later = head_copies(w_output, w_send, me % 2 * (w_send.shape[0] // 128), 1, late_sems)
    for copy in copies + later:
        copy.start()
    copies[0].wait()
    first = me * prior_keys.shape[0]

    def look(i, found):
        slot = table_s[i] - first
        return jnp.where((slot >= 0) & (slot < prior_keys.shape[0]), slot, found)

    slot = lax.fori_loop(0, table.shape[0], look, 0)
    pages = [
        pltpu.make_async_copy(prior_keys.at[slot], prior.at[:, :128], sems.at[8]),
        pltpu.make_async_copy(prior_values.at[slot], prior.at[:, 128:], sems.at[9]),
    ]
    for copy in pages:
        copy.start()
    for copy in copies[1:4]:
        copy.wait()
    row = lax.broadcasted_iota(jnp.int32, (BLOCK, 128), 0)
    lane = lanes_of((BLOCK, 128))
    for b in range(blocks):
        base = prior_len + order_s[me * blocks + b] * BLOCK
        angle = (base + row).astype(F32) * freq_v[...]
        part = pl.ds(b * BLOCK, BLOCK)
        sine = jnp.sin(angle)
        cos_out[part, :] = jnp.cos(angle)
        sin_out[part, :] = jnp.where(lane % 64 < 32, -sine, sine)
    for copy in copies[4:6]:
        copy.wait()
    wide = hidden_v[...].astype(F32)
    mean = jnp.mean(wide * wide, axis=-1, keepdims=True)
    normed = (wide * lax.rsqrt(mean + EPS) * gain_v[...]).astype(BF16)
    normed_out[...] = normed
    for copy in copies[6:]:
        copy.wait()
    keys = jnp.dot(normed, w_key_v[...], preferred_element_type=F32)
    values = jnp.dot(normed, w_value_v[...], preferred_element_type=F32)
    rotated = norm_and_rotate(keys, twice(key_gain_v), cos_out[...], sin_out[...])
    kv[:, :128] = rotated.astype(BF16)
    kv[:, 128:] = values.astype(BF16)
    for copy in pages + later:
        copy.wait()


def head_copies(w_output, target, first, other, sems):
    group = w_output.shape[0] // 128
    copies = []
    for i in range(target.shape[0] // 64):
        head = (i % 2) * group + first + i // 2
        rows = pl.ds(pl.multiple_of(head * 64, 64), 64)
        source = w_output.at[rows, columns(target, other)]
        copies.append(
            pltpu.make_async_copy(source, target.at[i * 64 : (i + 1) * 64, :], sems.at[i])
        )
    return copies


def columns(ref, other):
    x = lax.axis_index("head")
    x = 1 - x if other else x
    return pl.ds(pl.multiple_of(x * ref.shape[1], ref.shape[1]), ref.shape[1])


def query_kernel(normed, cosine, sine, w_query, query_gain, q_out):
    rows = normed.shape[0]
    blocks = rows // BLOCK
    tiles = w_query.shape[1] // 128
    per_kv = tiles // 2
    group = 2 * per_kv
    queries = jnp.dot(normed[...], w_query[...], preferred_element_type=F32)
    gain = twice(query_gain)
    left = lanes_of((rows, 128)) < 64
    for t in range(tiles):
        kv_head, u = divmod(t, per_kv)
        x = norm_and_rotate(queries[:, t * 128 : (t + 1) * 128], gain, cosine[...], sine[...])
        x = x * (64**-0.5 * LOG2E)
        turned = pltpu.roll(x, 64, 1)
        pair = (x, turned) if kv_head == 0 else (turned, x)
        for odd, head in enumerate(pair):
            kept = jnp.where(left if kv_head == 0 else ~left, head, 0.0)
            high = kept.astype(BF16)
            low = (kept - high.astype(F32)).astype(BF16)
            both = jnp.concatenate([high, low], axis=-1)
            for b in range(blocks):
                at = ((kv_head * blocks + b) * group + 2 * u + odd) * BLOCK
                q_out[at : at + BLOCK, :] = both[b * BLOCK : (b + 1) * BLOCK, :]


def mask_kernel(
    blocks, order, live, masks, w_query, turn,
    own_bias, span_bias, w_query_out, order_s, live_s, masks_s, sems,
):
    pairs = [(order, order_s), (live, live_s), (masks, masks_s)]
    bring = pltpu.make_async_copy(w_query, w_query_out, sems.at[3])
    bring.start()
    copies = [pltpu.make_async_copy(a, b, sems.at[i]) for i, (a, b) in enumerate(pairs)]
    for copy in copies:
        copy.start()
    for copy in copies:
        copy.wait()
    me = lax.axis_index("seq")
    logical = [order_s[me * blocks + b] for b in range(blocks)]
    key_at = lanes_of((BLOCK, blocks * BLOCK))
    row = lax.broadcasted_iota(jnp.int32, key_at.shape, 0)
    for b in range(blocks):
        bias = jnp.full(key_at.shape, MASKED, F32)
        for kb in range(blocks):
            alive = live_s[logical[kb]] > 0
            here = key_at // BLOCK == kb
            if kb == b:
                here = here & (key_at % BLOCK <= row)
            else:
                alive = alive & (logical[kb] < logical[b])
            bias = jnp.where(here, jnp.where(alive, 0.0, MASKED), bias)
        own_bias[b * BLOCK : (b + 1) * BLOCK, :] = bias

    count = masks.shape[0]
    lane = lanes_of((1, PAGE))

    def visit(i, carry):
        rank = me ^ masks_s[i]
        held = [order_s[rank * 2 + half] for half in range(2)]
        alive = [(live_s[block] > 0) & (rank != me) for block in held]
        for b in range(blocks):
            value = [
                jnp.where(alive[h] & (held[h] < logical[b]), 0.0, MASKED) for h in range(2)
            ]
            at = pl.ds(pl.multiple_of(i * PAGE, PAGE), PAGE)
            span_bias[b : b + 1, at] = jnp.where(lane < BLOCK, value[0], value[1])
        return carry

    lax.fori_loop(0, count, visit, 0, unroll=count <= 16)
    bring.wait()


class Piece:
    def __init__(self, rows, biases):
        keys, values = rows[:, :128], rows[:, 128:]
        left = lanes_of(values.shape) < 64
        ones = jnp.ones_like(values)
        self.keys = jnp.concatenate([keys, keys], axis=-1)
        self.values = [jnp.where(left, values, ones), jnp.where(left, ones, values)]
        self.biases = biases


def fold(q, m_in, acc_in, m_out, acc_out, pieces, blocks, part, finish=None):
    tiles = 2 * blocks
    scores, weights, totals = {}, {}, {}

    def score(t):
        rows = pl.ds(t * part, part)
        scores[t] = []
        for piece in pieces:
            s = lax.dot_general(
                q[rows, :], piece.keys, (((1,), (1,)), ((), ())), preferred_element_type=F32
            )
            scores[t].append(s if piece.biases is None else s + piece.biases[t % blocks])

    def weigh(t):
        rows = pl.ds(t * part, part)
        top = functools.reduce(jnp.maximum, [jnp.max(s, -1, keepdims=True) for s in scores[t]])
        factor = None
        if m_in is not None:
            old = m_in[rows, :1]
            top = jnp.maximum(top, old)
            factor = jnp.exp2(old - top)
        if finish is None:
            m_out[rows, :] = jnp.broadcast_to(top, (part, 128))
        weights[t] = [jnp.exp2(s - top).astype(BF16) for s in scores[t]], factor
        del scores[t]

    def mix(t):
        rows = pl.ds(t * part, part)
        parts, factor = weights.pop(t)
        total = 0.0 if factor is None else acc_in[rows, :] * factor
        for p, piece in zip(parts, pieces):
            total = total + jnp.dot(p, piece.values[t // blocks], preferred_element_type=F32)
        if finish is None:
            acc_out[rows, :] = total
            return
        totals[t] = total
        if t >= blocks:
            finish(t - blocks, totals.pop(t - blocks), totals.pop(t))

    score(0)
    for t in range(tiles + 1):
        if t + 1 < tiles:
            score(t + 1)
        if t < tiles:
            weigh(t)
        if t > 0:
            mix(t - 1)


def attention_kernel(offsets, own, first, last, step, blocks, group, *refs):
    refs = list(refs)
    q = refs.pop(0)
    own_kv, own_bias = (refs.pop(0), refs.pop(0)) if own else (None, None)
    chunks = [refs.pop(0) for _ in offsets]
    bias = refs.pop(0)
    m_in, acc_in = (None, None) if first else (refs.pop(0), refs.pop(0))
    out = refs.pop(0) if last else None
    m_ref, acc_ref = refs.pop(0), refs.pop(0)
    part = group * BLOCK

    def piece(rows, at):
        if at is None:
            return Piece(rows, None)
        size = rows.shape[0]
        return Piece(rows, [bias[b : b + 1, pl.ds(at, size)] for b in range(blocks)])

    extra = []
    if own:
        mine = [own_bias[b * BLOCK : (b + 1) * BLOCK, :] for b in range(blocks)]
        extra = [Piece(own_kv[...], [jnp.concatenate([m] * group, axis=0) for m in mine])]

    def finish(b, first_acc, second_acc):
        left = lanes_of(first_acc.shape) < 64
        top = jnp.where(left, first_acc, second_acc)
        sums = jnp.where(left, second_acc, first_acc)
        high = sums.astype(BF16)
        low = (sums - high.astype(F32)).astype(BF16)
        to = lax.broadcasted_iota(jnp.int32, (256, 128), 1)
        of = lax.broadcasted_iota(jnp.int32, (256, 128), 0)
        swapped = jnp.where(of % 128 == (to + 64) % 128, 1.0, 0.0).astype(BF16)
        sums = jnp.dot(
            jnp.concatenate([high, low], axis=-1), swapped, preferred_element_type=F32
        )
        ratio = (top / sums).astype(BF16)
        for u in range(group):
            out[b * BLOCK : (b + 1) * BLOCK, u * 128 : (u + 1) * 128] = ratio[
                u * BLOCK : (u + 1) * BLOCK, :
            ]

    if not refs:
        pieces = [piece(chunk[...], at) for chunk, at in zip(chunks, offsets)]
        fold(
            q, m_in, acc_in, m_ref, acc_ref, pieces + extra, blocks, part, finish if last else None
        )
        return
    held, sem = refs
    if own:
        fold(q, m_in, acc_in, m_ref, acc_ref, extra, blocks, part)
    elif not first:
        m_ref[...] = m_in[...]
        acc_ref[...] = acc_in[...]
    for chunk, at in zip(chunks, offsets):

        def visit(c, chunk=chunk, at=at):
            first_row = pl.multiple_of(c * step, step)
            copy = pltpu.make_async_copy(chunk.at[pl.ds(first_row, step)], held, sem)
            copy.start()
            copy.wait()
            pieces = [piece(held[...], None if at is None else at + first_row)]
            fold(q, m_ref, acc_ref, m_ref, acc_ref, pieces, blocks, part)

        pl.loop(0, chunk.shape[0] // step)(visit)
    if last:
        tiles = [acc_ref[t * part : (t + 1) * part, :] for t in range(2 * blocks)]
        for b in range(blocks):
            finish(b, tiles[b], tiles[blocks + b])


def attention(q, own, chunks, bias, state, last, blocks, group):
    arrays, offsets = zip(*chunks)
    rows = sum(c.shape[0] for c in arrays)
    direct = rows <= 2048
    step = min(1024, *(c.shape[0] for c in arrays))
    first = state is None
    operands = [q, *(own or ()), *arrays, bias, *(state or ())]
    specs = [spec(VMEM)] * len(operands)
    if not direct:
        at = 1 + len(own or ())
        specs[at : at + len(arrays)] = [spec(pl.ANY)] * len(arrays)
    n = q.shape[0]
    pair = [jax.ShapeDtypeStruct((n, 128), F32)] * 2
    scratch = []
    if not direct:
        scratch = [VMEM((step, 256), BF16), pltpu.SemaphoreType.DMA]
    if last:
        outs = jax.ShapeDtypeStruct((blocks * BLOCK, 2 * group * 64), BF16)
        out_specs = spec(VMEM)
        scratch = [VMEM((n, 128), F32)] * 2 + scratch
    else:
        outs, out_specs = pair, [spec(VMEM)] * 2
    return pl.pallas_call(
        functools.partial(
            attention_kernel, offsets, own is not None, first, last, step, blocks, group
        ),
        out_shape=outs,
        in_specs=specs,
        out_specs=out_specs,
        scratch_shapes=scratch,
        compiler_params=params(32),
        cost_estimate=cost(4 * n * rows * 256, rows * 512 + n * 2048),
    )(*operands)


def pages_kernel(n_chunks, dest, order, where, mine, w_output, *refs):
    chunks, (keys, values, partial, w_mine, sems, head_sems) = refs[:n_chunks], refs[n_chunks:]
    me = lax.axis_index("seq")
    copies = head_copies(w_output, w_mine, 0, 0, head_sems)
    for copy in copies:
        copy.start()

    def find(table):
        def body(wanted):
            return lax.fori_loop(
                0, table.shape[0], lambda i, f: jnp.where(table[i] == wanted, i, f), 0
            )

        return body

    page = find(dest)(me)
    for half in range(2):
        source = find(order)(page * 2 + half)
        slot = where[me ^ (source // 2)]
        row = slot * PAGE + (source % 2) * BLOCK
        at = 0
        for chunk in chunks:
            size = chunk.shape[0]
            inside = (row >= at) & (row < at + size)

            @pl.when(inside)
            def _(chunk=chunk, at=at):
                rows = pl.ds(pl.multiple_of(row - at, BLOCK), BLOCK)
                to = pl.ds(half * BLOCK, BLOCK)
                a = pltpu.make_async_copy(chunk.at[rows, :128], keys.at[0, to], sems.at[0])
                b = pltpu.make_async_copy(chunk.at[rows, 128:], values.at[0, to], sems.at[1])
                a.start()
                b.start()
                a.wait()
                b.wait()

            at += size
    for copy in copies:
        copy.wait()
    partial[...] = jnp.dot(mine[...], w_mine[...], preferred_element_type=F32)


def project_kernel(partial, peer, w_near, w_far, out):
    even = lax.axis_index("seq") % 2 == 0
    depth = w_near.shape[0]
    low, high = peer[:, :depth], peer[:, depth:]
    near = jnp.where(even, low, high)
    far = jnp.where(even, high, low)
    total = partial[...] + jnp.dot(near, w_near[...], preferred_element_type=F32)
    out[...] = total + jnp.dot(far, w_far[...], preferred_element_type=F32)


def plan(n):
    bits = [1 << i for i in range(n.bit_length() - 2, 0, -1)]
    return bits, bits[-1:] + bits[:-1]


def slot_masks(steps):
    masks = [0]
    for step in steps + [1]:
        masks = masks + [m ^ step for m in masks]
    return np.array(masks, np.int32)


def swap(x, n, step):
    return lax.ppermute(x, "seq", [(i, i ^ step) for i in range(n)])


def grow(held, n, step):
    return jnp.concatenate([held, swap(held, n, step)], axis=0)


def after(x, *others):
    return lax.optimization_barrier((x, *others))[0]


def body(
    n,
    hidden_in,
    attn_gain,
    w_query,
    w_key,
    w_value,
    query_gain,
    key_gain,
    w_output,
    prior_keys,
    prior_values,
    span_order,
    key_live,
    page_table,
    page_dest,
):
    rows, width = hidden_in.shape
    blocks = rows // BLOCK
    head_dim = query_gain.shape[0]
    group = w_query.shape[1] // w_key.shape[1]
    prior_len = page_table.shape[0] * PAGE
    out_width = w_output.shape[1] // 2
    depth = w_output.shape[0] // 2
    steps, span_steps = plan(n)
    masks = slot_masks(span_steps)
    where = np.zeros_like(masks)
    where[masks] = np.arange(n)
    half = head_dim // 2
    freq = np.tile((10000.0 ** (-np.arange(half) / half)).astype(np.float32), 4)[None, :]

    kv, prior, normed, cosine, sine, w_send = pl.pallas_call(
        functools.partial(kv_kernel, prior_len),
        out_shape=[
            jax.ShapeDtypeStruct((rows, 256), BF16),
            jax.ShapeDtypeStruct((PAGE, 256), BF16),
            jax.ShapeDtypeStruct((rows, width), BF16),
            jax.ShapeDtypeStruct((rows, 128), F32),
            jax.ShapeDtypeStruct((rows, 128), F32),
            jax.ShapeDtypeStruct((depth, out_width), BF16),
        ],
        in_specs=[spec(pltpu.HBM)] * 11,
        out_specs=[spec(VMEM)] * 6,
        scratch_shapes=[
            SMEM(span_order.shape, jnp.int32),
            SMEM(page_table.shape, jnp.int32),
            VMEM(hidden_in.shape, BF16),
            VMEM((1, width), F32),
            VMEM(w_key.shape, BF16),
            VMEM(w_value.shape, BF16),
            VMEM((1, head_dim), F32),
            VMEM((1, 128), F32),
            pltpu.SemaphoreType.DMA((10,)),
            pltpu.SemaphoreType.DMA((depth // 64,)),
        ],
        compiler_params=params(),
        cost_estimate=cost(2 * rows * width * 256, 3 << 20),
    )(
        *in_hbm(
            span_order,
            page_table,
            hidden_in,
            attn_gain.reshape(1, -1),
            w_key,
            w_value,
            key_gain.reshape(1, -1),
            jnp.asarray(freq),
            prior_keys,
            prior_values,
            w_output,
        )
    )

    with jax.named_scope("prior_step_0"):
        prior = grow(prior, n, steps[0])
    with jax.named_scope("span_step_0"):
        span = grow(kv, n, span_steps[0])
    normed = after(normed, prior, span)
    with jax.named_scope("weights_step"):
        w_near = lax.ppermute(w_send, "head", [(0, 1), (1, 0)])
        w_far = swap(w_near, n, 1)
    own_bias, span_bias, w_query = pl.pallas_call(
        functools.partial(mask_kernel, blocks),
        out_shape=[
            jax.ShapeDtypeStruct((rows, rows), F32),
            jax.ShapeDtypeStruct((blocks, n * PAGE), F32),
            jax.ShapeDtypeStruct(w_query.shape, BF16),
        ],
        in_specs=[spec(pltpu.HBM)] * 4 + [spec(pl.ANY)],
        out_specs=[spec(VMEM)] * 3,
        scratch_shapes=[
            SMEM(span_order.shape, jnp.int32),
            SMEM(key_live.shape, jnp.int32),
            SMEM((masks.size,), jnp.int32),
            pltpu.SemaphoreType.DMA((4,)),
        ],
        compiler_params=params(),
        cost_estimate=cost(1 << 28, 1 << 20),
    )(*in_hbm(span_order, key_live, jnp.asarray(masks), w_query), normed)
    q = pl.pallas_call(
        query_kernel,
        out_shape=jax.ShapeDtypeStruct((2 * blocks * group * BLOCK, 256), BF16),
        in_specs=[spec(VMEM)] * 5,
        out_specs=spec(VMEM),
        compiler_params=params(),
        cost_estimate=cost(2 * rows * width * 512, 4 << 20),
    )(normed, cosine, sine, w_query, query_gain.reshape(1, -1))
    for i, step in enumerate(steps[1:-1], 1):
        with jax.named_scope(f"prior_step_{i}"):
            prior = grow(prior, n, step)
        with jax.named_scope(f"span_step_{i}"):
            span = grow(span, n, span_steps[i])
    prior, span, _ = lax.optimization_barrier((prior, span, q))
    with jax.named_scope("prior_last"):
        prior_far = swap(prior, n, steps[-1])
    with jax.named_scope("span_last"):
        span_far = swap(span, n, span_steps[-1])
    prior, span = after(prior, own_bias), after(span, own_bias)
    with jax.named_scope("prior_core_near"):
        prior_core = swap(prior, n, 1)
    with jax.named_scope("span_core_near"):
        span_core = swap(span, n, 1)

    common = dict(bias=span_bias, blocks=blocks, group=group)
    part = n // 4 * PAGE
    chunks = [(prior, None), (span, 0)]
    state = attention(q, (kv, own_bias), chunks, state=None, last=False, **common)
    prior_far, span_far, *state = lax.optimization_barrier((prior_far, span_far, *state))
    with jax.named_scope("prior_core_far"):
        prior_core_far = swap(prior_far, n, 1)
    with jax.named_scope("span_core_far"):
        span_core_far = swap(span_far, n, 1)
    chunks = [(prior_far, None), (span_far, part), (prior_core, None), (span_core, 2 * part)]
    state = attention(q, None, chunks, state=state, last=False, **common)
    chunks = [(prior_core_far, None), (span_core_far, 3 * part)]
    heads = attention(q, None, chunks, state=state, last=True, **common)
    peer = lax.ppermute(heads, "head", [(0, 1), (1, 0)])

    all_span = [span, span_far, span_core, span_core_far]
    new_keys, new_values, partial = pl.pallas_call(
        functools.partial(pages_kernel, len(all_span)),
        out_shape=[jax.ShapeDtypeStruct((1, PAGE, 128), BF16)] * 2
        + [jax.ShapeDtypeStruct((rows, out_width), F32)],
        in_specs=[spec(SMEM)] * 3 + [spec(VMEM), spec(pltpu.HBM)] + [spec(pl.ANY)] * len(all_span),
        out_specs=[spec(VMEM)] * 3,
        scratch_shapes=[
            VMEM((w_output.shape[0], out_width), BF16),
            pltpu.SemaphoreType.DMA((2,)),
            pltpu.SemaphoreType.DMA((w_output.shape[0] // 64,)),
        ],
        compiler_params=params(),
        cost_estimate=cost(2 * rows * 512 * out_width, 1 << 21),
    )(page_dest, span_order, jnp.asarray(where), heads, *in_hbm(w_output), *all_span)

    attn_out = pl.pallas_call(
        project_kernel,
        out_shape=jax.ShapeDtypeStruct((rows, out_width), F32),
        in_specs=[spec(VMEM)] * 4,
        out_specs=spec(VMEM),
        compiler_params=params(),
        cost_estimate=cost(2 * rows * 512 * out_width, 2 << 20),
    )(partial, peer, w_near, w_far)
    return attn_out, new_keys, new_values


def solution(mesh):
    return jax.shard_map(
        functools.partial(body, mesh.shape["seq"]),
        mesh=mesh,
        in_specs=(
            P("seq", None),
            P(),
            P(None, "head"),
            P(None, "head"),
            P(None, "head"),
            P(),
            P(),
            P("head", None),
            P("seq", None, "head"),
            P("seq", None, "head"),
            P(),
            P(),
            P(),
            P(),
        ),
        out_specs=(P("seq", "head"), P("seq", None, "head"), P("seq", None, "head")),
        check_vma=False,
    )
```

```python
import functools

import jax
import jax.numpy as jnp
import numpy as np
from jax import lax
from jax.experimental import pallas as pl
from jax.experimental.pallas import tpu as pltpu
from jax.sharding import PartitionSpec as P

PAGE = 128
BLOCK = 64
EPS = 1e-06
MASKED = -1e30
F32 = jnp.float32
BF16 = jnp.bfloat16
VMEM = pltpu.VMEM
SMEM = pltpu.SMEM
LOG2E = 1.4426950408889634


def spec(space):
    return pl.BlockSpec(memory_space=space)


def in_hbm(*arrays):
    return [pltpu.with_memory_space_constraint(a, pltpu.HBM) for a in arrays]


def params(mib=32):
    return pltpu.CompilerParams(vmem_limit_bytes=mib * 1024 * 1024)


def cost(flops, size):
    return pl.CostEstimate(flops=int(flops), bytes_accessed=int(size), transcendentals=0)


def lanes_of(shape):
    return lax.broadcasted_iota(jnp.int32, shape, len(shape) - 1)


def norm_and_rotate(x, gain, cosine, sine):
    lane = lanes_of(x.shape)
    left = lane < 64
    square = x * x
    sum_left = jnp.sum(jnp.where(left, square, 0.0), axis=-1, keepdims=True)
    sum_right = jnp.sum(jnp.where(left, 0.0, square), axis=-1, keepdims=True)
    mean = jnp.where(left, sum_left, sum_right) * (1.0 / 64)
    y = x * lax.rsqrt(mean + EPS) * gain
    swapped = jnp.where(lane % 64 < 32, pltpu.roll(y, 96, 1), pltpu.roll(y, 32, 1))
    return y * cosine + swapped * sine


def twice(gain_ref):
    gain = gain_ref[...]
    return jnp.concatenate([gain, gain], axis=-1)


def kv_kernel(
    prior_len, order, table, hidden, gain, w_key, w_value, key_gain, freq, prior_keys, prior_values,
    w_output,
    kv, prior, normed_out, cos_out, sin_out, w_send,
    order_s, table_s, hidden_v, gain_v, w_key_v, w_value_v, key_gain_v, freq_v, sems, late_sems,
):
    rows = hidden.shape[0]
    blocks = rows // BLOCK
    me = lax.axis_index("seq")
    pairs = [
        (table, table_s), (order, order_s), (freq, freq_v), (key_gain, key_gain_v),
        (gain, gain_v), (hidden, hidden_v), (w_key, w_key_v), (w_value, w_value_v),
    ]
    copies = [pltpu.make_async_copy(a, b, sems.at[i]) for i, (a, b) in enumerate(pairs)]
    later = head_copies(w_output, w_send, me % 2 * (w_send.shape[0] // 128), 1, late_sems)
    for copy in copies + later:
        copy.start()
    copies[0].wait()
    first = me * prior_keys.shape[0]

    def look(i, found):
        slot = table_s[i] - first
        return jnp.where((slot >= 0) & (slot < prior_keys.shape[0]), slot, found)

    slot = lax.fori_loop(0, table.shape[0], look, 0)
    pages = [
        pltpu.make_async_copy(prior_keys.at[slot], prior.at[:, :128], sems.at[8]),
        pltpu.make_async_copy(prior_values.at[slot], prior.at[:, 128:], sems.at[9]),
    ]
    for copy in pages:
        copy.start()
    for copy in copies[1:4]:
        copy.wait()
    row = lax.broadcasted_iota(jnp.int32, (BLOCK, 128), 0)
    lane = lanes_of((BLOCK, 128))
    for b in range(blocks):
        base = prior_len + order_s[me * blocks + b] * BLOCK
        angle = (base + row).astype(F32) * freq_v[...]
        part = pl.ds(b * BLOCK, BLOCK)
        sine = jnp.sin(angle)
        cos_out[part, :] = jnp.cos(angle)
        sin_out[part, :] = jnp.where(lane % 64 < 32, -sine, sine)
    for copy in copies[4:6]:
        copy.wait()
    wide = hidden_v[...].astype(F32)
    mean = jnp.mean(wide * wide, axis=-1, keepdims=True)
    normed = (wide * lax.rsqrt(mean + EPS) * gain_v[...]).astype(BF16)
    normed_out[...] = normed
    for copy in copies[6:]:
        copy.wait()
    keys = jnp.dot(normed, w_key_v[...], preferred_element_type=F32)
    values = jnp.dot(normed, w_value_v[...], preferred_element_type=F32)
    rotated = norm_and_rotate(keys, twice(key_gain_v), cos_out[...], sin_out[...])
    kv[:, :128] = rotated.astype(BF16)
    kv[:, 128:] = values.astype(BF16)
    for copy in pages + later:
        copy.wait()


def head_copies(w_output, target, first, other, sems):
    group = w_output.shape[0] // 128
    copies = []
    for i in range(target.shape[0] // 64):
        head = (i % 2) * group + first + i // 2
        rows = pl.ds(pl.multiple_of(head * 64, 64), 64)
        source = w_output.at[rows, columns(target, other)]
        copies.append(
            pltpu.make_async_copy(source, target.at[i * 64 : (i + 1) * 64, :], sems.at[i])
        )
    return copies


def columns(ref, other):
    x = lax.axis_index("head")
    x = 1 - x if other else x
    return pl.ds(pl.multiple_of(x * ref.shape[1], ref.shape[1]), ref.shape[1])


def query_kernel(normed, cosine, sine, w_query, query_gain, q_out):
    rows = normed.shape[0]
    blocks = rows // BLOCK
    tiles = w_query.shape[1] // 128
    per_kv = tiles // 2
    group = 2 * per_kv
    queries = jnp.dot(normed[...], w_query[...], preferred_element_type=F32)
    gain = twice(query_gain)
    left = lanes_of((rows, 128)) < 64
    for t in range(tiles):
        kv_head, u = divmod(t, per_kv)
        x = norm_and_rotate(queries[:, t * 128 : (t + 1) * 128], gain, cosine[...], sine[...])
        x = x * (64**-0.5 * LOG2E)
        turned = pltpu.roll(x, 64, 1)
        pair = (x, turned) if kv_head == 0 else (turned, x)
        for odd, head in enumerate(pair):
            kept = jnp.where(left if kv_head == 0 else ~left, head, 0.0)
            high = kept.astype(BF16)
            low = (kept - high.astype(F32)).astype(BF16)
            both = jnp.concatenate([high, low], axis=-1)
            for b in range(blocks):
                at = ((kv_head * blocks + b) * group + 2 * u + odd) * BLOCK
                q_out[at : at + BLOCK, :] = both[b * BLOCK : (b + 1) * BLOCK, :]


def mask_kernel(
    blocks, order, live, masks, w_query, turn,
    own_bias, span_bias, w_query_out, order_s, live_s, masks_s, sems,
):
    pairs = [(order, order_s), (live, live_s), (masks, masks_s)]
    bring = pltpu.make_async_copy(w_query, w_query_out, sems.at[3])
    bring.start()
    copies = [pltpu.make_async_copy(a, b, sems.at[i]) for i, (a, b) in enumerate(pairs)]
    for copy in copies:
        copy.start()
    for copy in copies:
        copy.wait()
    me = lax.axis_index("seq")
    logical = [order_s[me * blocks + b] for b in range(blocks)]
    key_at = lanes_of((BLOCK, blocks * BLOCK))
    row = lax.broadcasted_iota(jnp.int32, key_at.shape, 0)
    for b in range(blocks):
        bias = jnp.full(key_at.shape, MASKED, F32)
        for kb in range(blocks):
            alive = live_s[logical[kb]] > 0
            here = key_at // BLOCK == kb
            if kb == b:
                here = here & (key_at % BLOCK <= row)
            else:
                alive = alive & (logical[kb] < logical[b])
            bias = jnp.where(here, jnp.where(alive, 0.0, MASKED), bias)
        own_bias[b * BLOCK : (b + 1) * BLOCK, :] = bias

    count = masks.shape[0]
    lane = lanes_of((1, PAGE))

    def visit(i, carry):
        rank = me ^ masks_s[i]
        held = [order_s[rank * 2 + half] for half in range(2)]
        alive = [(live_s[block] > 0) & (rank != me) for block in held]
        for b in range(blocks):
            value = [
                jnp.where(alive[h] & (held[h] < logical[b]), 0.0, MASKED) for h in range(2)
            ]
            at = pl.ds(pl.multiple_of(i * PAGE, PAGE), PAGE)
            span_bias[b : b + 1, at] = jnp.where(lane < BLOCK, value[0], value[1])
        return carry

    lax.fori_loop(0, count, visit, 0, unroll=count <= 16)
    bring.wait()


class Piece:
    def __init__(self, rows, biases):
        keys, values = rows[:, :128], rows[:, 128:]
        left = lanes_of(values.shape) < 64
        ones = jnp.ones_like(values)
        self.keys = jnp.concatenate([keys, keys], axis=-1)
        self.values = [jnp.where(left, values, ones), jnp.where(left, ones, values)]
        self.biases = biases


def fold(q, m_in, acc_in, m_out, acc_out, pieces, blocks, part, finish=None):
    tiles = 2 * blocks
    scores, weights, totals = {}, {}, {}

    def score(t):
        rows = pl.ds(t * part, part)
        scores[t] = []
        for piece in pieces:
            s = lax.dot_general(
                q[rows, :], piece.keys, (((1,), (1,)), ((), ())), preferred_element_type=F32
            )
            scores[t].append(s if piece.biases is None else s + piece.biases[t % blocks])

    def weigh(t):
        rows = pl.ds(t * part, part)
        top = functools.reduce(jnp.maximum, [jnp.max(s, -1, keepdims=True) for s in scores[t]])
        factor = None
        if m_in is not None:
            old = m_in[rows, :1]
            top = jnp.maximum(top, old)
            factor = jnp.exp2(old - top)
        if finish is None:
            m_out[rows, :] = jnp.broadcast_to(top, (part, 128))
        weights[t] = [jnp.exp2(s - top).astype(BF16) for s in scores[t]], factor
        del scores[t]

    def mix(t):
        rows = pl.ds(t * part, part)
        parts, factor = weights.pop(t)
        total = 0.0 if factor is None else acc_in[rows, :] * factor
        for p, piece in zip(parts, pieces):
            total = total + jnp.dot(p, piece.values[t // blocks], preferred_element_type=F32)
        if finish is None:
            acc_out[rows, :] = total
            return
        totals[t] = total
        if t >= blocks:
            finish(t - blocks, totals.pop(t - blocks), totals.pop(t))

    score(0)
    for t in range(tiles + 1):
        if t + 1 < tiles:
            score(t + 1)
        if t < tiles:
            weigh(t)
        if t > 0:
            mix(t - 1)


def attention_kernel(offsets, join, own, first, last, step, blocks, group, *refs):
    refs = list(refs)
    q = refs.pop(0)
    own_kv, own_bias = (refs.pop(0), refs.pop(0)) if own else (None, None)
    chunks = [refs.pop(0) for _ in offsets]
    bias = refs.pop(0)
    m_in, acc_in = (None, None) if first else (refs.pop(0), refs.pop(0))
    out = refs.pop(0) if last else None
    m_ref, acc_ref = refs.pop(0), refs.pop(0)
    part = group * BLOCK

    def piece(rows, at):
        if at is None:
            return Piece(rows, None)
        size = rows.shape[0]
        return Piece(rows, [bias[b : b + 1, pl.ds(at, size)] for b in range(blocks)])

    extra = []
    if own:
        mine = [own_bias[b * BLOCK : (b + 1) * BLOCK, :] for b in range(blocks)]
        extra = [Piece(own_kv[...], [jnp.concatenate([m] * group, axis=0) for m in mine])]

    def finish(b, first_acc, second_acc):
        left = lanes_of(first_acc.shape) < 64
        top = jnp.where(left, first_acc, second_acc)
        sums = jnp.where(left, second_acc, first_acc)
        high = sums.astype(BF16)
        low = (sums - high.astype(F32)).astype(BF16)
        to = lax.broadcasted_iota(jnp.int32, (256, 128), 1)
        of = lax.broadcasted_iota(jnp.int32, (256, 128), 0)
        swapped = jnp.where(of % 128 == (to + 64) % 128, 1.0, 0.0).astype(BF16)
        sums = jnp.dot(
            jnp.concatenate([high, low], axis=-1), swapped, preferred_element_type=F32
        )
        ratio = (top / sums).astype(BF16)
        for u in range(group):
            out[b * BLOCK : (b + 1) * BLOCK, u * 128 : (u + 1) * 128] = ratio[
                u * BLOCK : (u + 1) * BLOCK, :
            ]

    if not refs:
        rows = [chunk[...] for chunk in chunks]
        starts = range(0, len(rows), join)
        pieces = [piece(jnp.concatenate(rows[i : i + join], axis=0), offsets[i]) for i in starts]
        fold(
            q, m_in, acc_in, m_ref, acc_ref, pieces + extra, blocks, part, finish if last else None
        )
        return
    held, sem = refs
    if own:
        fold(q, m_in, acc_in, m_ref, acc_ref, extra, blocks, part)
    elif not first:
        m_ref[...] = m_in[...]
        acc_ref[...] = acc_in[...]
    for chunk, at in zip(chunks, offsets):

        def visit(c, chunk=chunk, at=at):
            first_row = pl.multiple_of(c * step, step)
            copy = pltpu.make_async_copy(chunk.at[pl.ds(first_row, step)], held, sem)
            copy.start()
            copy.wait()
            pieces = [piece(held[...], None if at is None else at + first_row)]
            fold(q, m_ref, acc_ref, m_ref, acc_ref, pieces, blocks, part)

        pl.loop(0, chunk.shape[0] // step)(visit)
    if last:
        tiles = [acc_ref[t * part : (t + 1) * part, :] for t in range(2 * blocks)]
        for b in range(blocks):
            finish(b, tiles[b], tiles[blocks + b])


def attention(q, own, chunks, bias, state, last, blocks, group, join=1):
    arrays, offsets = zip(*chunks)
    rows = sum(c.shape[0] for c in arrays)
    direct = rows <= 2048
    step = min(1024, *(c.shape[0] for c in arrays))
    first = state is None
    operands = [q, *(own or ()), *arrays, bias, *(state or ())]
    specs = [spec(VMEM)] * len(operands)
    if not direct:
        at = 1 + len(own or ())
        specs[at : at + len(arrays)] = [spec(pl.ANY)] * len(arrays)
    n = q.shape[0]
    pair = [jax.ShapeDtypeStruct((n, 128), F32)] * 2
    scratch = []
    if not direct:
        scratch = [VMEM((step, 256), BF16), pltpu.SemaphoreType.DMA]
    if last:
        outs = jax.ShapeDtypeStruct((blocks * BLOCK, 2 * group * 64), BF16)
        out_specs = spec(VMEM)
        scratch = [VMEM((n, 128), F32)] * 2 + scratch
    else:
        outs, out_specs = pair, [spec(VMEM)] * 2
    return pl.pallas_call(
        functools.partial(
            attention_kernel, offsets, join, own is not None, first, last, step, blocks, group
        ),
        out_shape=outs,
        in_specs=specs,
        out_specs=out_specs,
        scratch_shapes=scratch,
        compiler_params=params(32),
        cost_estimate=cost(1000, 1000) if first or join > 1 else cost(4 * n * rows * 256, rows * 512 + n * 2048),
    )(*operands)


def pages_kernel(n_chunks, dest, order, where, mine, w_output, *refs):
    chunks, (keys, values, partial, w_mine, sems, head_sems) = refs[:n_chunks], refs[n_chunks:]
    me = lax.axis_index("seq")
    copies = head_copies(w_output, w_mine, 0, 0, head_sems)
    for copy in copies:
        copy.start()

    def find(table):
        def body(wanted):
            return lax.fori_loop(
                0, table.shape[0], lambda i, f: jnp.where(table[i] == wanted, i, f), 0
            )

        return body

    page = find(dest)(me)
    for half in range(2):
        source = find(order)(page * 2 + half)
        slot = where[me ^ (source // 2)]
        row = slot * PAGE + (source % 2) * BLOCK
        at = 0
        for chunk in chunks:
            size = chunk.shape[0]
            inside = (row >= at) & (row < at + size)

            @pl.when(inside)
            def _(chunk=chunk, at=at):
                rows = pl.ds(pl.multiple_of(row - at, BLOCK), BLOCK)
                to = pl.ds(half * BLOCK, BLOCK)
                a = pltpu.make_async_copy(chunk.at[rows, :128], keys.at[0, to], sems.at[0])
                b = pltpu.make_async_copy(chunk.at[rows, 128:], values.at[0, to], sems.at[1])
                a.start()
                b.start()
                a.wait()
                b.wait()

            at += size
    for copy in copies:
        copy.wait()
    partial[...] = jnp.dot(mine[...], w_mine[...], preferred_element_type=F32)


def project_kernel(partial, peer, w_near, w_far, out):
    even = lax.axis_index("seq") % 2 == 0
    depth = w_near.shape[0]
    low, high = peer[:, :depth], peer[:, depth:]
    near = jnp.where(even, low, high)
    far = jnp.where(even, high, low)
    total = partial[...] + jnp.dot(near, w_near[...], preferred_element_type=F32)
    out[...] = total + jnp.dot(far, w_far[...], preferred_element_type=F32)


def plan(n):
    bits = [1 << i for i in range(n.bit_length() - 2, 0, -1)]
    return bits, bits[-1:] + bits[:-1]


def slot_masks(steps):
    masks = [0]
    for step in steps + [1]:
        masks = masks + [m ^ step for m in masks]
    return np.array(masks, np.int32)


def swap(x, n, step):
    return lax.ppermute(x, "seq", [(i, i ^ step) for i in range(n)])


def grow(held, n, step):
    return jnp.concatenate([held, swap(held, n, step)], axis=0)


def after(x, *others):
    return lax.optimization_barrier((x, *others))[0]


def body(
    n,
    hidden_in,
    attn_gain,
    w_query,
    w_key,
    w_value,
    query_gain,
    key_gain,
    w_output,
    prior_keys,
    prior_values,
    span_order,
    key_live,
    page_table,
    page_dest,
):
    rows, width = hidden_in.shape
    blocks = rows // BLOCK
    head_dim = query_gain.shape[0]
    group = w_query.shape[1] // w_key.shape[1]
    prior_len = page_table.shape[0] * PAGE
    out_width = w_output.shape[1] // 2
    depth = w_output.shape[0] // 2
    steps, span_steps = plan(n)
    masks = slot_masks(span_steps)
    where = np.zeros_like(masks)
    where[masks] = np.arange(n)
    half = head_dim // 2
    freq = np.tile((10000.0 ** (-np.arange(half) / half)).astype(np.float32), 4)[None, :]

    kv, prior, normed, cosine, sine, w_send = pl.pallas_call(
        functools.partial(kv_kernel, prior_len),
        out_shape=[
            jax.ShapeDtypeStruct((rows, 256), BF16),
            jax.ShapeDtypeStruct((PAGE, 256), BF16),
            jax.ShapeDtypeStruct((rows, width), BF16),
            jax.ShapeDtypeStruct((rows, 128), F32),
            jax.ShapeDtypeStruct((rows, 128), F32),
            jax.ShapeDtypeStruct((depth, out_width), BF16),
        ],
        in_specs=[spec(pltpu.HBM)] * 11,
        out_specs=[spec(VMEM)] * 6,
        scratch_shapes=[
            SMEM(span_order.shape, jnp.int32),
            SMEM(page_table.shape, jnp.int32),
            VMEM(hidden_in.shape, BF16),
            VMEM((1, width), F32),
            VMEM(w_key.shape, BF16),
            VMEM(w_value.shape, BF16),
            VMEM((1, head_dim), F32),
            VMEM((1, 128), F32),
            pltpu.SemaphoreType.DMA((10,)),
            pltpu.SemaphoreType.DMA((depth // 64,)),
        ],
        compiler_params=params(),
        cost_estimate=cost(2 * rows * width * 256, 3 << 20),
    )(
        *in_hbm(
            span_order,
            page_table,
            hidden_in,
            attn_gain.reshape(1, -1),
            w_key,
            w_value,
            key_gain.reshape(1, -1),
            jnp.asarray(freq),
            prior_keys,
            prior_values,
            w_output,
        )
    )

    with jax.named_scope("prior_step_0"):
        prior = grow(prior, n, steps[0])
    with jax.named_scope("span_step_0"):
        span = grow(kv, n, span_steps[0])
    normed = after(normed, prior, span)
    with jax.named_scope("weights_step"):
        w_near = lax.ppermute(w_send, "head", [(0, 1), (1, 0)])
        w_far = swap(w_near, n, 1)
    own_bias, span_bias, w_query = pl.pallas_call(
        functools.partial(mask_kernel, blocks),
        out_shape=[
            jax.ShapeDtypeStruct((rows, rows), F32),
            jax.ShapeDtypeStruct((blocks, n * PAGE), F32),
            jax.ShapeDtypeStruct(w_query.shape, BF16),
        ],
        in_specs=[spec(pltpu.HBM)] * 4 + [spec(pl.ANY)],
        out_specs=[spec(VMEM)] * 3,
        scratch_shapes=[
            SMEM(span_order.shape, jnp.int32),
            SMEM(key_live.shape, jnp.int32),
            SMEM((masks.size,), jnp.int32),
            pltpu.SemaphoreType.DMA((4,)),
        ],
        compiler_params=params(),
        cost_estimate=cost(1 << 28, 1 << 20),
    )(*in_hbm(span_order, key_live, jnp.asarray(masks), w_query), normed)
    q = pl.pallas_call(
        query_kernel,
        out_shape=jax.ShapeDtypeStruct((2 * blocks * group * BLOCK, 256), BF16),
        in_specs=[spec(VMEM)] * 5,
        out_specs=spec(VMEM),
        compiler_params=params(),
        cost_estimate=cost(2 * rows * width * 512, 4 << 20),
    )(normed, cosine, sine, w_query, query_gain.reshape(1, -1))
    for i, step in enumerate(steps[1:-1], 1):
        with jax.named_scope(f"prior_step_{i}"):
            prior = grow(prior, n, step)
        with jax.named_scope(f"span_step_{i}"):
            span = grow(span, n, span_steps[i])
    prior, span, _ = lax.optimization_barrier((prior, span, q))
    with jax.named_scope("prior_last"):
        prior_far = swap(prior, n, steps[-1])
    with jax.named_scope("span_last"):
        span_far = swap(span, n, span_steps[-1])
    prior, span = after(prior, own_bias), after(span, own_bias)
    half = prior.shape[0] // 2
    with jax.named_scope("prior_core_near"):
        prior_core = [swap(prior[:half], n, 1), swap(prior[half:], n, 1)]
    with jax.named_scope("span_core_near"):
        span_core = [swap(span[:half], n, 1), swap(span[half:], n, 1)]

    common = dict(bias=span_bias, blocks=blocks, group=group)
    part = n // 4 * PAGE
    chunks = [(prior, None), (span, 0)]
    state = attention(q, (kv, own_bias), chunks, state=None, last=False, **common)
    chunks = [(c, None) for c in prior_core]
    chunks += [(c, 2 * part + i * half) for i, c in enumerate(span_core)]
    state = attention(q, None, chunks, state=state, last=False, join=2, **common)
    prior_far, span_far, *state = lax.optimization_barrier((prior_far, span_far, *state))
    with jax.named_scope("prior_core_far"):
        prior_core_far = swap(prior_far, n, 1)
    with jax.named_scope("span_core_far"):
        span_core_far = swap(span_far, n, 1)
    chunks = [(prior_far, None), (span_far, part)]
    state = attention(q, None, chunks, state=state, last=False, **common)
    chunks = [(prior_core_far, None), (span_core_far, 3 * part)]
    heads = attention(q, None, chunks, state=state, last=True, **common)
    peer = lax.ppermute(heads, "head", [(0, 1), (1, 0)])

    all_span = [span, span_far, *span_core, span_core_far]
    new_keys, new_values, partial = pl.pallas_call(
        functools.partial(pages_kernel, len(all_span)),
        out_shape=[jax.ShapeDtypeStruct((1, PAGE, 128), BF16)] * 2
        + [jax.ShapeDtypeStruct((rows, out_width), F32)],
        in_specs=[spec(SMEM)] * 3 + [spec(VMEM), spec(pltpu.HBM)] + [spec(pl.ANY)] * len(all_span),
        out_specs=[spec(VMEM)] * 3,
        scratch_shapes=[
            VMEM((w_output.shape[0], out_width), BF16),
            pltpu.SemaphoreType.DMA((2,)),
            pltpu.SemaphoreType.DMA((w_output.shape[0] // 64,)),
        ],
        compiler_params=params(),
        cost_estimate=cost(2 * rows * 512 * out_width, 1 << 21),
    )(page_dest, span_order, jnp.asarray(where), heads, *in_hbm(w_output), *all_span)

    attn_out = pl.pallas_call(
        project_kernel,
        out_shape=jax.ShapeDtypeStruct((rows, out_width), F32),
        in_specs=[spec(VMEM)] * 4,
        out_specs=spec(VMEM),
        compiler_params=params(),
        cost_estimate=cost(2 * rows * 512 * out_width, 2 << 20),
    )(partial, peer, w_near, w_far)
    return attn_out, new_keys, new_values


def solution(mesh):
    return jax.shard_map(
        functools.partial(body, mesh.shape["seq"]),
        mesh=mesh,
        in_specs=(
            P("seq", None),
            P(),
            P(None, "head"),
            P(None, "head"),
            P(None, "head"),
            P(),
            P(),
            P("head", None),
            P("seq", None, "head"),
            P("seq", None, "head"),
            P(),
            P(),
            P(),
            P(),
        ),
        out_specs=(P("seq", "head"), P("seq", None, "head"), P("seq", None, "head")),
        check_vma=False,
    )
```

```python
import functools

import jax
import jax.numpy as jnp
import numpy as np
from jax import lax
from jax.experimental import pallas as pl
from jax.experimental.pallas import tpu as pltpu
from jax.sharding import PartitionSpec as P

PAGE = 128
BLOCK = 64
EPS = 1e-06
MASKED = -1e30
F32 = jnp.float32
BF16 = jnp.bfloat16
VMEM = pltpu.VMEM
SMEM = pltpu.SMEM
LOG2E = 1.4426950408889634


def spec(space):
    return pl.BlockSpec(memory_space=space)


def in_hbm(*arrays):
    return [pltpu.with_memory_space_constraint(a, pltpu.HBM) for a in arrays]


def params(mib=32):
    return pltpu.CompilerParams(vmem_limit_bytes=mib * 1024 * 1024)


def cost(flops, size):
    return pl.CostEstimate(flops=int(flops), bytes_accessed=int(size), transcendentals=0)


def lanes_of(shape):
    return lax.broadcasted_iota(jnp.int32, shape, len(shape) - 1)


def norm_and_rotate(x, gain, cosine, sine):
    lane = lanes_of(x.shape)
    left = lane < 64
    square = x * x
    sum_left = jnp.sum(jnp.where(left, square, 0.0), axis=-1, keepdims=True)
    sum_right = jnp.sum(jnp.where(left, 0.0, square), axis=-1, keepdims=True)
    mean = jnp.where(left, sum_left, sum_right) * (1.0 / 64)
    y = x * lax.rsqrt(mean + EPS) * gain
    swapped = jnp.where(lane % 64 < 32, pltpu.roll(y, 96, 1), pltpu.roll(y, 32, 1))
    return y * cosine + swapped * sine


def twice(gain_ref):
    gain = gain_ref[...]
    return jnp.concatenate([gain, gain], axis=-1)


def kv_kernel(
    prior_len, order, table, hidden, gain, w_key, w_value, key_gain, freq, prior_keys, prior_values,
    w_output,
    kv, prior, normed_out, cos_out, sin_out, w_send,
    order_s, table_s, hidden_v, gain_v, w_key_v, w_value_v, key_gain_v, freq_v, sems, late_sems,
):
    rows = hidden.shape[0]
    blocks = rows // BLOCK
    me = lax.axis_index("seq")
    pairs = [
        (table, table_s), (order, order_s), (freq, freq_v), (key_gain, key_gain_v),
        (gain, gain_v), (hidden, hidden_v), (w_key, w_key_v), (w_value, w_value_v),
    ]
    copies = [pltpu.make_async_copy(a, b, sems.at[i]) for i, (a, b) in enumerate(pairs)]
    later = head_copies(w_output, w_send, me % 2 * (w_send.shape[0] // 128), 1, late_sems)
    for copy in copies + later:
        copy.start()
    copies[0].wait()
    first = me * prior_keys.shape[0]

    def look(i, found):
        slot = table_s[i] - first
        return jnp.where((slot >= 0) & (slot < prior_keys.shape[0]), slot, found)

    slot = lax.fori_loop(0, table.shape[0], look, 0)
    pages = [
        pltpu.make_async_copy(prior_keys.at[slot], prior.at[:, :128], sems.at[8]),
        pltpu.make_async_copy(prior_values.at[slot], prior.at[:, 128:], sems.at[9]),
    ]
    for copy in pages:
        copy.start()
    for copy in copies[1:4]:
        copy.wait()
    row = lax.broadcasted_iota(jnp.int32, (BLOCK, 128), 0)
    lane = lanes_of((BLOCK, 128))
    for b in range(blocks):
        base = prior_len + order_s[me * blocks + b] * BLOCK
        angle = (base + row).astype(F32) * freq_v[...]
        part = pl.ds(b * BLOCK, BLOCK)
        sine = jnp.sin(angle)
        cos_out[part, :] = jnp.cos(angle)
        sin_out[part, :] = jnp.where(lane % 64 < 32, -sine, sine)
    for copy in copies[4:6]:
        copy.wait()
    wide = hidden_v[...].astype(F32)
    mean = jnp.mean(wide * wide, axis=-1, keepdims=True)
    normed = (wide * lax.rsqrt(mean + EPS) * gain_v[...]).astype(BF16)
    normed_out[...] = normed
    for copy in copies[6:]:
        copy.wait()
    keys = jnp.dot(normed, w_key_v[...], preferred_element_type=F32)
    values = jnp.dot(normed, w_value_v[...], preferred_element_type=F32)
    rotated = norm_and_rotate(keys, twice(key_gain_v), cos_out[...], sin_out[...])
    kv[:, :128] = rotated.astype(BF16)
    kv[:, 128:] = values.astype(BF16)
    for copy in pages + later:
        copy.wait()


def head_copies(w_output, target, first, other, sems):
    group = w_output.shape[0] // 128
    copies = []
    for i in range(target.shape[0] // 64):
        head = (i % 2) * group + first + i // 2
        rows = pl.ds(pl.multiple_of(head * 64, 64), 64)
        source = w_output.at[rows, columns(target, other)]
        copies.append(
            pltpu.make_async_copy(source, target.at[i * 64 : (i + 1) * 64, :], sems.at[i])
        )
    return copies


def columns(ref, other):
    x = lax.axis_index("head")
    x = 1 - x if other else x
    return pl.ds(pl.multiple_of(x * ref.shape[1], ref.shape[1]), ref.shape[1])


def query_kernel(normed, cosine, sine, w_query, query_gain, q_out):
    rows = normed.shape[0]
    blocks = rows // BLOCK
    tiles = w_query.shape[1] // 128
    per_kv = tiles // 2
    group = 2 * per_kv
    queries = jnp.dot(normed[...], w_query[...], preferred_element_type=F32)
    gain = twice(query_gain)
    left = lanes_of((rows, 128)) < 64
    for t in range(tiles):
        kv_head, u = divmod(t, per_kv)
        x = norm_and_rotate(queries[:, t * 128 : (t + 1) * 128], gain, cosine[...], sine[...])
        x = x * (64**-0.5 * LOG2E)
        turned = pltpu.roll(x, 64, 1)
        pair = (x, turned) if kv_head == 0 else (turned, x)
        for odd, head in enumerate(pair):
            kept = jnp.where(left if kv_head == 0 else ~left, head, 0.0)
            high = kept.astype(BF16)
            low = (kept - high.astype(F32)).astype(BF16)
            both = jnp.concatenate([high, low], axis=-1)
            for b in range(blocks):
                at = ((kv_head * blocks + b) * group + 2 * u + odd) * BLOCK
                q_out[at : at + BLOCK, :] = both[b * BLOCK : (b + 1) * BLOCK, :]


def mask_kernel(
    blocks, order, live, masks, w_query, turn,
    own_bias, span_bias, w_query_out, order_s, live_s, masks_s, sems,
):
    pairs = [(order, order_s), (live, live_s), (masks, masks_s)]
    bring = pltpu.make_async_copy(w_query, w_query_out, sems.at[3])
    bring.start()
    copies = [pltpu.make_async_copy(a, b, sems.at[i]) for i, (a, b) in enumerate(pairs)]
    for copy in copies:
        copy.start()
    for copy in copies:
        copy.wait()
    me = lax.axis_index("seq")
    logical = [order_s[me * blocks + b] for b in range(blocks)]
    key_at = lanes_of((BLOCK, blocks * BLOCK))
    row = lax.broadcasted_iota(jnp.int32, key_at.shape, 0)
    for b in range(blocks):
        bias = jnp.full(key_at.shape, MASKED, F32)
        for kb in range(blocks):
            alive = live_s[logical[kb]] > 0
            here = key_at // BLOCK == kb
            if kb == b:
                here = here & (key_at % BLOCK <= row)
            else:
                alive = alive & (logical[kb] < logical[b])
            bias = jnp.where(here, jnp.where(alive, 0.0, MASKED), bias)
        own_bias[b * BLOCK : (b + 1) * BLOCK, :] = bias

    count = masks.shape[0]
    lane = lanes_of((1, PAGE))

    def visit(i, carry):
        rank = me ^ masks_s[i]
        held = [order_s[rank * 2 + half] for half in range(2)]
        alive = [(live_s[block] > 0) & (rank != me) for block in held]
        for b in range(blocks):
            value = [
                jnp.where(alive[h] & (held[h] < logical[b]), 0.0, MASKED) for h in range(2)
            ]
            at = pl.ds(pl.multiple_of(i * PAGE, PAGE), PAGE)
            span_bias[b : b + 1, at] = jnp.where(lane < BLOCK, value[0], value[1])
        return carry

    lax.fori_loop(0, count, visit, 0, unroll=count <= 16)
    bring.wait()


class Piece:
    def __init__(self, rows, biases):
        keys, values = rows[:, :128], rows[:, 128:]
        left = lanes_of(values.shape) < 64
        ones = jnp.ones_like(values)
        self.keys = jnp.concatenate([keys, keys], axis=-1)
        self.values = [jnp.where(left, values, ones), jnp.where(left, ones, values)]
        self.biases = biases


def fold(q, m_in, acc_in, m_out, acc_out, pieces, blocks, part, finish=None):
    tiles = 2 * blocks
    scores, weights, totals = {}, {}, {}

    def score(t):
        rows = pl.ds(t * part, part)
        scores[t] = []
        for piece in pieces:
            s = lax.dot_general(
                q[rows, :], piece.keys, (((1,), (1,)), ((), ())), preferred_element_type=F32
            )
            scores[t].append(s if piece.biases is None else s + piece.biases[t % blocks])

    def weigh(t):
        rows = pl.ds(t * part, part)
        top = functools.reduce(jnp.maximum, [jnp.max(s, -1, keepdims=True) for s in scores[t]])
        factor = None
        if m_in is not None:
            old = m_in[rows, :1]
            top = jnp.maximum(top, old)
            factor = jnp.exp2(old - top)
        if finish is None:
            m_out[rows, :] = jnp.broadcast_to(top, (part, 128))
        weights[t] = [jnp.exp2(s - top).astype(BF16) for s in scores[t]], factor
        del scores[t]

    def mix(t):
        rows = pl.ds(t * part, part)
        parts, factor = weights.pop(t)
        total = 0.0 if factor is None else acc_in[rows, :] * factor
        for p, piece in zip(parts, pieces):
            total = total + jnp.dot(p, piece.values[t // blocks], preferred_element_type=F32)
        if finish is None:
            acc_out[rows, :] = total
            return
        totals[t] = total
        if t >= blocks:
            finish(t - blocks, totals.pop(t - blocks), totals.pop(t))

    score(0)
    for t in range(tiles + 1):
        if t + 1 < tiles:
            score(t + 1)
        if t < tiles:
            weigh(t)
        if t > 0:
            mix(t - 1)


def attention_kernel(offsets, join, own, first, last, step, blocks, group, *refs):
    refs = list(refs)
    q = refs.pop(0)
    own_kv, own_bias = (refs.pop(0), refs.pop(0)) if own else (None, None)
    chunks = [refs.pop(0) for _ in offsets]
    bias = refs.pop(0)
    m_in, acc_in = (None, None) if first else (refs.pop(0), refs.pop(0))
    out = refs.pop(0) if last else None
    m_ref, acc_ref = refs.pop(0), refs.pop(0)
    part = group * BLOCK

    def piece(rows, at):
        if at is None:
            return Piece(rows, None)
        size = rows.shape[0]
        return Piece(rows, [bias[b : b + 1, pl.ds(at, size)] for b in range(blocks)])

    extra = []
    if own:
        mine = [own_bias[b * BLOCK : (b + 1) * BLOCK, :] for b in range(blocks)]
        extra = [Piece(own_kv[...], [jnp.concatenate([m] * group, axis=0) for m in mine])]

    def finish(b, first_acc, second_acc):
        left = lanes_of(first_acc.shape) < 64
        top = jnp.where(left, first_acc, second_acc)
        sums = jnp.where(left, second_acc, first_acc)
        high = sums.astype(BF16)
        low = (sums - high.astype(F32)).astype(BF16)
        to = lax.broadcasted_iota(jnp.int32, (256, 128), 1)
        of = lax.broadcasted_iota(jnp.int32, (256, 128), 0)
        swapped = jnp.where(of % 128 == (to + 64) % 128, 1.0, 0.0).astype(BF16)
        sums = jnp.dot(
            jnp.concatenate([high, low], axis=-1), swapped, preferred_element_type=F32
        )
        ratio = (top / sums).astype(BF16)
        for u in range(group):
            out[b * BLOCK : (b + 1) * BLOCK, u * 128 : (u + 1) * 128] = ratio[
                u * BLOCK : (u + 1) * BLOCK, :
            ]

    if not refs:
        rows = [chunk[...] for chunk in chunks]
        starts = range(0, len(rows), join)
        pieces = []
        for i in starts:
            joined = jnp.concatenate(rows[i : i + join], axis=0)
            halves = offsets[i] if isinstance(offsets[i], tuple) else (offsets[i],)
            size = joined.shape[0] // len(halves)
            pieces += [piece(joined[h * size : (h + 1) * size, :], at) for h, at in enumerate(halves)]
        fold(
            q, m_in, acc_in, m_ref, acc_ref, pieces + extra, blocks, part, finish if last else None
        )
        return
    held, sem = refs
    if own:
        fold(q, m_in, acc_in, m_ref, acc_ref, extra, blocks, part)
    elif not first:
        m_ref[...] = m_in[...]
        acc_ref[...] = acc_in[...]
    for chunk, at in zip(chunks, offsets):
        halves = at if isinstance(at, tuple) else (at,)
        size = chunk.shape[0] // len(halves)
        for i, half in enumerate(halves):

            def visit(c, chunk=chunk, half=half, start=i * size):
                row = pl.multiple_of(c * step, step)
                copy = pltpu.make_async_copy(chunk.at[pl.ds(start + row, step)], held, sem)
                copy.start()
                copy.wait()
                pieces = [piece(held[...], None if half is None else half + row)]
                fold(q, m_ref, acc_ref, m_ref, acc_ref, pieces, blocks, part)

            pl.loop(0, size // step)(visit)
    if last:
        tiles = [acc_ref[t * part : (t + 1) * part, :] for t in range(2 * blocks)]
        for b in range(blocks):
            finish(b, tiles[b], tiles[blocks + b])


def attention(q, own, chunks, bias, state, last, blocks, group, join=1):
    arrays, offsets = zip(*chunks)
    rows = sum(c.shape[0] for c in arrays)
    direct = rows <= 2048
    step = min([1024] + [c.shape[0] // 2 for c in arrays])
    first = state is None
    operands = [q, *(own or ()), *arrays, bias, *(state or ())]
    specs = [spec(VMEM)] * len(operands)
    if not direct:
        at = 1 + len(own or ())
        specs[at : at + len(arrays)] = [spec(pl.ANY)] * len(arrays)
    n = q.shape[0]
    pair = [jax.ShapeDtypeStruct((n, 128), F32)] * 2
    scratch = []
    if not direct:
        scratch = [VMEM((step, 256), BF16), pltpu.SemaphoreType.DMA]
    if last:
        outs = jax.ShapeDtypeStruct((blocks * BLOCK, 2 * group * 64), BF16)
        out_specs = spec(VMEM)
        scratch = [VMEM((n, 128), F32)] * 2 + scratch
    else:
        outs, out_specs = pair, [spec(VMEM)] * 2
    return pl.pallas_call(
        functools.partial(
            attention_kernel, offsets, join, own is not None, first, last, step, blocks, group
        ),
        out_shape=outs,
        in_specs=specs,
        out_specs=out_specs,
        scratch_shapes=scratch,
        compiler_params=params(32),
        cost_estimate=cost(1000, 1000) if first or join > 1 else cost(4 * n * rows * 256, rows * 512 + n * 2048),
    )(*operands)


def pages_kernel(n_chunks, dest, order, where, mine, w_output, *refs):
    chunks, (keys, values, partial, w_mine, sems, head_sems) = refs[:n_chunks], refs[n_chunks:]
    me = lax.axis_index("seq")
    copies = head_copies(w_output, w_mine, 0, 0, head_sems)
    for copy in copies:
        copy.start()

    def find(table):
        def body(wanted):
            return lax.fori_loop(
                0, table.shape[0], lambda i, f: jnp.where(table[i] == wanted, i, f), 0
            )

        return body

    page = find(dest)(me)
    for half in range(2):
        source = find(order)(page * 2 + half)
        slot = where[me ^ (source // 2)]
        row = slot * PAGE + (source % 2) * BLOCK
        at = 0
        for chunk in chunks:
            size = min(chunk.shape[0], chunks[0].shape[0])
            inside = (row >= at) & (row < at + size)

            @pl.when(inside)
            def _(chunk=chunk, at=at - (chunk.shape[0] - size)):
                rows = pl.ds(pl.multiple_of(row - at, BLOCK), BLOCK)
                to = pl.ds(half * BLOCK, BLOCK)
                a = pltpu.make_async_copy(chunk.at[rows, :128], keys.at[0, to], sems.at[0])
                b = pltpu.make_async_copy(chunk.at[rows, 128:], values.at[0, to], sems.at[1])
                a.start()
                b.start()
                a.wait()
                b.wait()

            at += size
    for copy in copies:
        copy.wait()
    partial[...] = jnp.dot(mine[...], w_mine[...], preferred_element_type=F32)


def project_kernel(partial, peer, w_near, w_far, out):
    even = lax.axis_index("seq") % 2 == 0
    depth = w_near.shape[0]
    low, high = peer[:, :depth], peer[:, depth:]
    near = jnp.where(even, low, high)
    far = jnp.where(even, high, low)
    total = partial[...] + jnp.dot(near, w_near[...], preferred_element_type=F32)
    out[...] = total + jnp.dot(far, w_far[...], preferred_element_type=F32)


def plan(n):
    bits = [1 << i for i in range(n.bit_length() - 2, 0, -1)]
    return bits, bits[-1:] + bits[:-1]


def slot_masks(steps):
    masks = [0]
    for step in steps + [1]:
        masks = masks + [m ^ step for m in masks]
    return np.array(masks, np.int32)


def swap(x, n, step):
    return lax.ppermute(x, "seq", [(i, i ^ step) for i in range(n)])


def grow(held, n, step):
    return jnp.concatenate([held, swap(held, n, step)], axis=0)


def after(x, *others):
    return lax.optimization_barrier((x, *others))[0]


def body(
    n,
    hidden_in,
    attn_gain,
    w_query,
    w_key,
    w_value,
    query_gain,
    key_gain,
    w_output,
    prior_keys,
    prior_values,
    span_order,
    key_live,
    page_table,
    page_dest,
):
    rows, width = hidden_in.shape
    blocks = rows // BLOCK
    head_dim = query_gain.shape[0]
    group = w_query.shape[1] // w_key.shape[1]
    prior_len = page_table.shape[0] * PAGE
    out_width = w_output.shape[1] // 2
    depth = w_output.shape[0] // 2
    steps, span_steps = plan(n)
    masks = slot_masks(span_steps)
    where = np.zeros_like(masks)
    where[masks] = np.arange(n)
    half = head_dim // 2
    freq = np.tile((10000.0 ** (-np.arange(half) / half)).astype(np.float32), 4)[None, :]

    kv, prior, normed, cosine, sine, w_send = pl.pallas_call(
        functools.partial(kv_kernel, prior_len),
        out_shape=[
            jax.ShapeDtypeStruct((rows, 256), BF16),
            jax.ShapeDtypeStruct((PAGE, 256), BF16),
            jax.ShapeDtypeStruct((rows, width), BF16),
            jax.ShapeDtypeStruct((rows, 128), F32),
            jax.ShapeDtypeStruct((rows, 128), F32),
            jax.ShapeDtypeStruct((depth, out_width), BF16),
        ],
        in_specs=[spec(pltpu.HBM)] * 11,
        out_specs=[spec(VMEM)] * 6,
        scratch_shapes=[
            SMEM(span_order.shape, jnp.int32),
            SMEM(page_table.shape, jnp.int32),
            VMEM(hidden_in.shape, BF16),
            VMEM((1, width), F32),
            VMEM(w_key.shape, BF16),
            VMEM(w_value.shape, BF16),
            VMEM((1, head_dim), F32),
            VMEM((1, 128), F32),
            pltpu.SemaphoreType.DMA((10,)),
            pltpu.SemaphoreType.DMA((depth // 64,)),
        ],
        compiler_params=params(),
        cost_estimate=cost(2 * rows * width * 256, 3 << 20),
    )(
        *in_hbm(
            span_order,
            page_table,
            hidden_in,
            attn_gain.reshape(1, -1),
            w_key,
            w_value,
            key_gain.reshape(1, -1),
            jnp.asarray(freq),
            prior_keys,
            prior_values,
            w_output,
        )
    )

    with jax.named_scope("prior_step_0"):
        prior = grow(prior, n, steps[0])
    with jax.named_scope("span_step_0"):
        span = grow(kv, n, span_steps[0])
    normed = after(normed, prior, span)
    with jax.named_scope("weights_step"):
        w_near = lax.ppermute(w_send, "head", [(0, 1), (1, 0)])
        w_far = swap(w_near, n, 1)
    own_bias, span_bias, w_query = pl.pallas_call(
        functools.partial(mask_kernel, blocks),
        out_shape=[
            jax.ShapeDtypeStruct((rows, rows), F32),
            jax.ShapeDtypeStruct((blocks, n * PAGE), F32),
            jax.ShapeDtypeStruct(w_query.shape, BF16),
        ],
        in_specs=[spec(pltpu.HBM)] * 4 + [spec(pl.ANY)],
        out_specs=[spec(VMEM)] * 3,
        scratch_shapes=[
            SMEM(span_order.shape, jnp.int32),
            SMEM(key_live.shape, jnp.int32),
            SMEM((masks.size,), jnp.int32),
            pltpu.SemaphoreType.DMA((4,)),
        ],
        compiler_params=params(),
        cost_estimate=cost(1 << 28, 1 << 20),
    )(*in_hbm(span_order, key_live, jnp.asarray(masks), w_query), normed)
    q = pl.pallas_call(
        query_kernel,
        out_shape=jax.ShapeDtypeStruct((2 * blocks * group * BLOCK, 256), BF16),
        in_specs=[spec(VMEM)] * 5,
        out_specs=spec(VMEM),
        compiler_params=params(),
        cost_estimate=cost(2 * rows * width * 512, 4 << 20),
    )(normed, cosine, sine, w_query, query_gain.reshape(1, -1))
    for i, step in enumerate(steps[1:-1], 1):
        with jax.named_scope(f"prior_step_{i}"):
            prior = grow(prior, n, step)
        with jax.named_scope(f"span_step_{i}"):
            span = grow(span, n, span_steps[i])
    prior, span, _ = lax.optimization_barrier((prior, span, q))
    with jax.named_scope("prior_last"):
        prior_far = swap(prior, n, steps[-1])
    with jax.named_scope("span_last"):
        span_far = swap(span, n, span_steps[-1])
    prior, span = after(prior, own_bias), after(span, own_bias)
    half = prior.shape[0] // 2
    with jax.named_scope("prior_core_near"):
        prior_core = [swap(prior[:half], n, 1), swap(prior[half:], n, 1)]
    with jax.named_scope("span_core_near"):
        span_core = [swap(span[:half], n, 1), swap(span[half:], n, 1)]

    common = dict(bias=span_bias, blocks=blocks, group=group)
    part = n // 4 * PAGE
    chunks = [(prior, None), (span, 0)]
    state = attention(q, (kv, own_bias), chunks, state=None, last=False, **common)
    chunks = [(c, None) for c in prior_core]
    chunks += [(c, 2 * part + i * half) for i, c in enumerate(span_core)]
    state = attention(q, None, chunks, state=state, last=False, join=2, **common)
    prior_far, span_far, *state = lax.optimization_barrier((prior_far, span_far, *state))
    with jax.named_scope("core_far"):
        far_core = swap(jnp.concatenate([prior_far, span_far], axis=0), n, 1)
    chunks = [(prior_far, None), (span_far, part)]
    state = attention(q, None, chunks, state=state, last=False, **common)
    chunks = [(far_core, (None, 3 * part))]
    heads = attention(q, None, chunks, state=state, last=True, **common)
    peer = lax.ppermute(heads, "head", [(0, 1), (1, 0)])

    all_span = [span, span_far, *span_core, far_core]
    new_keys, new_values, partial = pl.pallas_call(
        functools.partial(pages_kernel, len(all_span)),
        out_shape=[jax.ShapeDtypeStruct((1, PAGE, 128), BF16)] * 2
        + [jax.ShapeDtypeStruct((rows, out_width), F32)],
        in_specs=[spec(SMEM)] * 3 + [spec(VMEM), spec(pltpu.HBM)] + [spec(pl.ANY)] * len(all_span),
        out_specs=[spec(VMEM)] * 3,
        scratch_shapes=[
            VMEM((w_output.shape[0], out_width), BF16),
            pltpu.SemaphoreType.DMA((2,)),
            pltpu.SemaphoreType.DMA((w_output.shape[0] // 64,)),
        ],
        compiler_params=params(),
        cost_estimate=cost(2 * rows * 512 * out_width, 1 << 21),
    )(page_dest, span_order, jnp.asarray(where), heads, *in_hbm(w_output), *all_span)

    attn_out = pl.pallas_call(
        project_kernel,
        out_shape=jax.ShapeDtypeStruct((rows, out_width), F32),
        in_specs=[spec(VMEM)] * 4,
        out_specs=spec(VMEM),
        compiler_params=params(),
        cost_estimate=cost(2 * rows * 512 * out_width, 2 << 20),
    )(partial, peer, w_near, w_far)
    return attn_out, new_keys, new_values


def solution(mesh):
    return jax.shard_map(
        functools.partial(body, mesh.shape["seq"]),
        mesh=mesh,
        in_specs=(
            P("seq", None),
            P(),
            P(None, "head"),
            P(None, "head"),
            P(None, "head"),
            P(),
            P(),
            P("head", None),
            P("seq", None, "head"),
            P("seq", None, "head"),
            P(),
            P(),
            P(),
            P(),
        ),
        out_specs=(P("seq", "head"), P("seq", None, "head"), P("seq", None, "head")),
        check_vma=False,
    )
```

```python
import functools

import jax
import jax.numpy as jnp
import numpy as np
from jax import lax
from jax.experimental import pallas as pl
from jax.experimental.pallas import tpu as pltpu
from jax.sharding import PartitionSpec as P

PAGE = 128
BLOCK = 64
EPS = 1e-06
MASKED = -1e30
F32 = jnp.float32
BF16 = jnp.bfloat16
VMEM = pltpu.VMEM
SMEM = pltpu.SMEM
LOG2E = 1.4426950408889634


def spec(space):
    return pl.BlockSpec(memory_space=space)


def in_hbm(*arrays):
    return [pltpu.with_memory_space_constraint(a, pltpu.HBM) for a in arrays]


def params(mib=32):
    return pltpu.CompilerParams(vmem_limit_bytes=mib * 1024 * 1024)


def cost(flops, size):
    return pl.CostEstimate(flops=int(flops), bytes_accessed=int(size), transcendentals=0)


def lanes_of(shape):
    return lax.broadcasted_iota(jnp.int32, shape, len(shape) - 1)


def norm_and_rotate(x, gain, cosine, sine):
    lane = lanes_of(x.shape)
    left = lane < 64
    square = x * x
    sum_left = jnp.sum(jnp.where(left, square, 0.0), axis=-1, keepdims=True)
    sum_right = jnp.sum(jnp.where(left, 0.0, square), axis=-1, keepdims=True)
    mean = jnp.where(left, sum_left, sum_right) * (1.0 / 64)
    y = x * lax.rsqrt(mean + EPS) * gain
    swapped = jnp.where(lane % 64 < 32, pltpu.roll(y, 96, 1), pltpu.roll(y, 32, 1))
    return y * cosine + swapped * sine


def twice(gain_ref):
    gain = gain_ref[...]
    return jnp.concatenate([gain, gain], axis=-1)


def kv_kernel(
    prior_len, order, table, hidden, gain, w_key, w_value, key_gain, freq, prior_keys, prior_values,
    w_output,
    kv, prior, normed_out, cos_out, sin_out, w_send,
    order_s, table_s, hidden_v, gain_v, w_key_v, w_value_v, key_gain_v, freq_v, sems, late_sems,
):
    rows = hidden.shape[0]
    blocks = rows // BLOCK
    me = lax.axis_index("seq")
    pairs = [
        (table, table_s), (order, order_s), (freq, freq_v), (key_gain, key_gain_v),
        (gain, gain_v), (hidden, hidden_v), (w_key, w_key_v), (w_value, w_value_v),
    ]
    copies = [pltpu.make_async_copy(a, b, sems.at[i]) for i, (a, b) in enumerate(pairs)]
    later = head_copies(w_output, w_send, me % 2 * (w_send.shape[0] // 128), 1, late_sems)
    for copy in copies + later:
        copy.start()
    copies[0].wait()
    first = me * prior_keys.shape[0]

    def look(i, found):
        slot = table_s[i] - first
        return jnp.where((slot >= 0) & (slot < prior_keys.shape[0]), slot, found)

    slot = lax.fori_loop(0, table.shape[0], look, 0)
    pages = [
        pltpu.make_async_copy(prior_keys.at[slot], prior.at[:, :128], sems.at[8]),
        pltpu.make_async_copy(prior_values.at[slot], prior.at[:, 128:], sems.at[9]),
    ]
    for copy in pages:
        copy.start()
    for copy in copies[1:4]:
        copy.wait()
    row = lax.broadcasted_iota(jnp.int32, (BLOCK, 128), 0)
    lane = lanes_of((BLOCK, 128))
    for b in range(blocks):
        base = prior_len + order_s[me * blocks + b] * BLOCK
        angle = (base + row).astype(F32) * freq_v[...]
        part = pl.ds(b * BLOCK, BLOCK)
        sine = jnp.sin(angle)
        cos_out[part, :] = jnp.cos(angle)
        sin_out[part, :] = jnp.where(lane % 64 < 32, -sine, sine)
    for copy in copies[4:6]:
        copy.wait()
    wide = hidden_v[...].astype(F32)
    mean = jnp.mean(wide * wide, axis=-1, keepdims=True)
    normed = (wide * lax.rsqrt(mean + EPS) * gain_v[...]).astype(BF16)
    normed_out[...] = normed
    for copy in copies[6:]:
        copy.wait()
    keys = jnp.dot(normed, w_key_v[...], preferred_element_type=F32)
    values = jnp.dot(normed, w_value_v[...], preferred_element_type=F32)
    rotated = norm_and_rotate(keys, twice(key_gain_v), cos_out[...], sin_out[...])
    kv[:, :128] = rotated.astype(BF16)
    kv[:, 128:] = values.astype(BF16)
    for copy in pages + later:
        copy.wait()


def head_copies(w_output, target, first, other, sems):
    group = w_output.shape[0] // 128
    copies = []
    for i in range(target.shape[0] // 64):
        head = (i % 2) * group + first + i // 2
        rows = pl.ds(pl.multiple_of(head * 64, 64), 64)
        source = w_output.at[rows, columns(target, other)]
        copies.append(
            pltpu.make_async_copy(source, target.at[i * 64 : (i + 1) * 64, :], sems.at[i])
        )
    return copies


def columns(ref, other):
    x = lax.axis_index("head")
    x = 1 - x if other else x
    return pl.ds(pl.multiple_of(x * ref.shape[1], ref.shape[1]), ref.shape[1])


def query_kernel(
    normed, cosine, sine, w_query, query_gain, order, live, masks,
    q_out, own_bias, span_bias, w_query_v, query_gain_v, order_s, live_s, masks_s, sems, tile_sems,
):
    bring = []
    for t in range(w_query.shape[1] // 256):
        at = slice(t * 256, (t + 1) * 256)
        bring.append(
            pltpu.make_async_copy(w_query.at[:, at], w_query_v.at[:, at], tile_sems.at[t])
        )
    pairs = [(order, order_s), (live, live_s), (masks, masks_s), (query_gain, query_gain_v)]
    copies = [pltpu.make_async_copy(a, b, sems.at[i]) for i, (a, b) in enumerate(pairs)]
    for copy in copies + bring:
        copy.start()
    for copy in copies:
        copy.wait()
    fill_masks(normed.shape[0] // BLOCK, order_s, live_s, masks_s, own_bias, span_bias)
    rows = normed.shape[0]
    blocks = rows // BLOCK
    tiles = w_query.shape[1] // 128
    per_kv = tiles // 2
    group = 2 * per_kv
    gain = twice(query_gain_v)
    left = lanes_of((rows, 128)) < 64
    for t in range(tiles):
        kv_head, u = divmod(t, per_kv)
        if t % 2 == 0:
            bring[t // 2].wait()
            two = jnp.dot(
                normed[...], w_query_v[:, t * 128 : (t + 2) * 128], preferred_element_type=F32
            )
        x = two[:, t % 2 * 128 : (t % 2 + 1) * 128]
        x = norm_and_rotate(x, gain, cosine[...], sine[...])
        x = x * (64**-0.5 * LOG2E)
        turned = pltpu.roll(x, 64, 1)
        pair = (x, turned) if kv_head == 0 else (turned, x)
        for odd, head in enumerate(pair):
            kept = jnp.where(left if kv_head == 0 else ~left, head, 0.0)
            high = kept.astype(BF16)
            low = (kept - high.astype(F32)).astype(BF16)
            both = jnp.concatenate([high, low], axis=-1)
            for b in range(blocks):
                at = ((kv_head * blocks + b) * group + 2 * u + odd) * BLOCK
                q_out[at : at + BLOCK, :] = both[b * BLOCK : (b + 1) * BLOCK, :]


def fill_masks(blocks, order_s, live_s, masks_s, own_bias, span_bias):
    me = lax.axis_index("seq")
    logical = [order_s[me * blocks + b] for b in range(blocks)]
    key_at = lanes_of((BLOCK, blocks * BLOCK))
    row = lax.broadcasted_iota(jnp.int32, key_at.shape, 0)
    for b in range(blocks):
        bias = jnp.full(key_at.shape, MASKED, F32)
        for kb in range(blocks):
            alive = live_s[logical[kb]] > 0
            here = key_at // BLOCK == kb
            if kb == b:
                here = here & (key_at % BLOCK <= row)
            else:
                alive = alive & (logical[kb] < logical[b])
            bias = jnp.where(here, jnp.where(alive, 0.0, MASKED), bias)
        own_bias[b * BLOCK : (b + 1) * BLOCK, :] = bias

    count = masks_s.shape[0]
    lane = lanes_of((1, PAGE))

    def visit(i, carry):
        rank = me ^ masks_s[i]
        held = [order_s[rank * 2 + half] for half in range(2)]
        alive = [(live_s[block] > 0) & (rank != me) for block in held]
        for b in range(blocks):
            value = [
                jnp.where(alive[h] & (held[h] < logical[b]), 0.0, MASKED) for h in range(2)
            ]
            at = pl.ds(pl.multiple_of(i * PAGE, PAGE), PAGE)
            span_bias[b : b + 1, at] = jnp.where(lane < BLOCK, value[0], value[1])
        return carry

    lax.fori_loop(0, count, visit, 0, unroll=count <= 16)


class Piece:
    def __init__(self, rows, biases):
        keys, values = rows[:, :128], rows[:, 128:]
        left = lanes_of(values.shape) < 64
        ones = jnp.ones_like(values)
        self.keys = jnp.concatenate([keys, keys], axis=-1)
        self.values = [jnp.where(left, values, ones), jnp.where(left, ones, values)]
        self.biases = biases


def fold(q, m_in, acc_in, m_out, acc_out, pieces, blocks, part, finish=None):
    tiles = 2 * blocks
    scores, weights, totals = {}, {}, {}

    def score(t):
        rows = pl.ds(t * part, part)
        scores[t] = []
        for piece in pieces:
            s = lax.dot_general(
                q[rows, :], piece.keys, (((1,), (1,)), ((), ())), preferred_element_type=F32
            )
            scores[t].append(s if piece.biases is None else s + piece.biases[t % blocks])

    def weigh(t):
        rows = pl.ds(t * part, part)
        top = functools.reduce(jnp.maximum, [jnp.max(s, -1, keepdims=True) for s in scores[t]])
        factor = None
        if m_in is not None:
            old = m_in[rows, :1]
            top = jnp.maximum(top, old)
            factor = jnp.exp2(old - top)
        if finish is None:
            m_out[rows, :] = jnp.broadcast_to(top, (part, 128))
        weights[t] = [jnp.exp2(s - top).astype(BF16) for s in scores[t]], factor
        del scores[t]

    def mix(t):
        rows = pl.ds(t * part, part)
        parts, factor = weights.pop(t)
        total = 0.0 if factor is None else acc_in[rows, :] * factor
        for p, piece in zip(parts, pieces):
            total = total + jnp.dot(p, piece.values[t // blocks], preferred_element_type=F32)
        if finish is None:
            acc_out[rows, :] = total
            return
        totals[t] = total
        if t >= blocks:
            finish(t - blocks, totals.pop(t - blocks), totals.pop(t))

    score(0)
    for t in range(tiles + 1):
        if t + 1 < tiles:
            score(t + 1)
        if t < tiles:
            weigh(t)
        if t > 0:
            mix(t - 1)


def attention_kernel(offsets, join, own, first, last, step, blocks, group, *refs):
    refs = list(refs)
    q = refs.pop(0)
    own_kv, own_bias = (refs.pop(0), refs.pop(0)) if own else (None, None)
    chunks = [refs.pop(0) for _ in offsets]
    bias = refs.pop(0)
    m_in, acc_in = (None, None) if first else (refs.pop(0), refs.pop(0))
    out = refs.pop(0) if last else None
    m_ref, acc_ref = refs.pop(0), refs.pop(0)
    part = group * BLOCK

    def piece(rows, at):
        if at is None:
            return Piece(rows, None)
        size = rows.shape[0]
        return Piece(rows, [bias[b : b + 1, pl.ds(at, size)] for b in range(blocks)])

    extra = []
    if own:
        mine = [own_bias[b * BLOCK : (b + 1) * BLOCK, :] for b in range(blocks)]
        extra = [Piece(own_kv[...], [jnp.concatenate([m] * group, axis=0) for m in mine])]

    def finish(b, first_acc, second_acc):
        left = lanes_of(first_acc.shape) < 64
        top = jnp.where(left, first_acc, second_acc)
        sums = jnp.where(left, second_acc, first_acc)
        high = sums.astype(BF16)
        low = (sums - high.astype(F32)).astype(BF16)
        to = lax.broadcasted_iota(jnp.int32, (256, 128), 1)
        of = lax.broadcasted_iota(jnp.int32, (256, 128), 0)
        swapped = jnp.where(of % 128 == (to + 64) % 128, 1.0, 0.0).astype(BF16)
        sums = jnp.dot(
            jnp.concatenate([high, low], axis=-1), swapped, preferred_element_type=F32
        )
        ratio = (top / sums).astype(BF16)
        for u in range(group):
            out[b * BLOCK : (b + 1) * BLOCK, u * 128 : (u + 1) * 128] = ratio[
                u * BLOCK : (u + 1) * BLOCK, :
            ]

    if not refs:
        rows = [chunk[...] for chunk in chunks]
        starts = range(0, len(rows), join)
        pieces = []
        for i in starts:
            joined = jnp.concatenate(rows[i : i + join], axis=0)
            halves = offsets[i] if isinstance(offsets[i], tuple) else (offsets[i],)
            size = joined.shape[0] // len(halves)
            pieces += [piece(joined[h * size : (h + 1) * size, :], at) for h, at in enumerate(halves)]
        fold(
            q, m_in, acc_in, m_ref, acc_ref, pieces + extra, blocks, part, finish if last else None
        )
        return
    held, sem = refs
    if own:
        fold(q, m_in, acc_in, m_ref, acc_ref, extra, blocks, part)
    elif not first:
        m_ref[...] = m_in[...]
        acc_ref[...] = acc_in[...]
    for chunk, at in zip(chunks, offsets):
        halves = at if isinstance(at, tuple) else (at,)
        size = chunk.shape[0] // len(halves)
        for i, half in enumerate(halves):

            def visit(c, chunk=chunk, half=half, start=i * size):
                row = pl.multiple_of(c * step, step)
                copy = pltpu.make_async_copy(chunk.at[pl.ds(start + row, step)], held, sem)
                copy.start()
                copy.wait()
                pieces = [piece(held[...], None if half is None else half + row)]
                fold(q, m_ref, acc_ref, m_ref, acc_ref, pieces, blocks, part)

            pl.loop(0, size // step)(visit)
    if last:
        tiles = [acc_ref[t * part : (t + 1) * part, :] for t in range(2 * blocks)]
        for b in range(blocks):
            finish(b, tiles[b], tiles[blocks + b])


def attention(q, own, chunks, bias, state, last, blocks, group, join=1):
    arrays, offsets = zip(*chunks)
    rows = sum(c.shape[0] for c in arrays)
    direct = rows <= 2048
    step = min([1024] + [c.shape[0] // 2 for c in arrays])
    first = state is None
    operands = [q, *(own or ()), *arrays, bias, *(state or ())]
    specs = [spec(VMEM)] * len(operands)
    if not direct:
        at = 1 + len(own or ())
        specs[at : at + len(arrays)] = [spec(pl.ANY)] * len(arrays)
    n = q.shape[0]
    pair = [jax.ShapeDtypeStruct((n, 128), F32)] * 2
    scratch = []
    if not direct:
        scratch = [VMEM((step, 256), BF16), pltpu.SemaphoreType.DMA]
    if last:
        outs = jax.ShapeDtypeStruct((blocks * BLOCK, 2 * group * 64), BF16)
        out_specs = spec(VMEM)
        scratch = [VMEM((n, 128), F32)] * 2 + scratch
    else:
        outs, out_specs = pair, [spec(VMEM)] * 2
    return pl.pallas_call(
        functools.partial(
            attention_kernel, offsets, join, own is not None, first, last, step, blocks, group
        ),
        out_shape=outs,
        in_specs=specs,
        out_specs=out_specs,
        scratch_shapes=scratch,
        compiler_params=params(32),
        cost_estimate=cost(1000, 1000) if first or join > 1 else cost(4 * n * rows * 256, rows * 512 + n * 2048),
    )(*operands)


def pages_kernel(n_chunks, dest, order, where, mine, w_output, *refs):
    chunks, (keys, values, partial, w_mine, sems, head_sems) = refs[:n_chunks], refs[n_chunks:]
    me = lax.axis_index("seq")
    copies = head_copies(w_output, w_mine, 0, 0, head_sems)
    for copy in copies:
        copy.start()

    def find(table):
        def body(wanted):
            return lax.fori_loop(
                0, table.shape[0], lambda i, f: jnp.where(table[i] == wanted, i, f), 0
            )

        return body

    page = find(dest)(me)
    for half in range(2):
        source = find(order)(page * 2 + half)
        slot = where[me ^ (source // 2)]
        row = slot * PAGE + (source % 2) * BLOCK
        at = 0
        for chunk in chunks:
            size = min(chunk.shape[0], chunks[0].shape[0])
            inside = (row >= at) & (row < at + size)

            @pl.when(inside)
            def _(chunk=chunk, at=at - (chunk.shape[0] - size)):
                rows = pl.ds(pl.multiple_of(row - at, BLOCK), BLOCK)
                to = pl.ds(half * BLOCK, BLOCK)
                a = pltpu.make_async_copy(chunk.at[rows, :128], keys.at[0, to], sems.at[0])
                b = pltpu.make_async_copy(chunk.at[rows, 128:], values.at[0, to], sems.at[1])
                a.start()
                b.start()
                a.wait()
                b.wait()

            at += size
    for copy in copies:
        copy.wait()
    partial[...] = jnp.dot(mine[...], w_mine[...], preferred_element_type=F32)


def project_kernel(partial, peer, w_near, w_far, out):
    even = lax.axis_index("seq") % 2 == 0
    depth = w_near.shape[0]
    low, high = peer[:, :depth], peer[:, depth:]
    near = jnp.where(even, low, high)
    far = jnp.where(even, high, low)
    total = partial[...] + jnp.dot(near, w_near[...], preferred_element_type=F32)
    out[...] = total + jnp.dot(far, w_far[...], preferred_element_type=F32)


def plan(n):
    bits = [1 << i for i in range(n.bit_length() - 2, 0, -1)]
    return bits, bits[-1:] + bits[:-1]


def slot_masks(steps):
    masks = [0]
    for step in steps + [1]:
        masks = masks + [m ^ step for m in masks]
    return np.array(masks, np.int32)


def swap(x, n, step):
    return lax.ppermute(x, "seq", [(i, i ^ step) for i in range(n)])


def grow(held, n, step):
    return jnp.concatenate([held, swap(held, n, step)], axis=0)


def after(x, *others):
    return lax.optimization_barrier((x, *others))[0]


def body(
    n,
    hidden_in,
    attn_gain,
    w_query,
    w_key,
    w_value,
    query_gain,
    key_gain,
    w_output,
    prior_keys,
    prior_values,
    span_order,
    key_live,
    page_table,
    page_dest,
):
    rows, width = hidden_in.shape
    blocks = rows // BLOCK
    head_dim = query_gain.shape[0]
    group = w_query.shape[1] // w_key.shape[1]
    prior_len = page_table.shape[0] * PAGE
    out_width = w_output.shape[1] // 2
    depth = w_output.shape[0] // 2
    steps, span_steps = plan(n)
    masks = slot_masks(span_steps)
    where = np.zeros_like(masks)
    where[masks] = np.arange(n)
    half = head_dim // 2
    freq = np.tile((10000.0 ** (-np.arange(half) / half)).astype(np.float32), 4)[None, :]

    kv, prior, normed, cosine, sine, w_send = pl.pallas_call(
        functools.partial(kv_kernel, prior_len),
        out_shape=[
            jax.ShapeDtypeStruct((rows, 256), BF16),
            jax.ShapeDtypeStruct((PAGE, 256), BF16),
            jax.ShapeDtypeStruct((rows, width), BF16),
            jax.ShapeDtypeStruct((rows, 128), F32),
            jax.ShapeDtypeStruct((rows, 128), F32),
            jax.ShapeDtypeStruct((depth, out_width), BF16),
        ],
        in_specs=[spec(pltpu.HBM)] * 11,
        out_specs=[spec(VMEM)] * 6,
        scratch_shapes=[
            SMEM(span_order.shape, jnp.int32),
            SMEM(page_table.shape, jnp.int32),
            VMEM(hidden_in.shape, BF16),
            VMEM((1, width), F32),
            VMEM(w_key.shape, BF16),
            VMEM(w_value.shape, BF16),
            VMEM((1, head_dim), F32),
            VMEM((1, 128), F32),
            pltpu.SemaphoreType.DMA((10,)),
            pltpu.SemaphoreType.DMA((depth // 64,)),
        ],
        compiler_params=params(),
        cost_estimate=cost(2 * rows * width * 256, 3 << 20),
    )(
        *in_hbm(
            span_order,
            page_table,
            hidden_in,
            attn_gain.reshape(1, -1),
            w_key,
            w_value,
            key_gain.reshape(1, -1),
            jnp.asarray(freq),
            prior_keys,
            prior_values,
            w_output,
        )
    )

    with jax.named_scope("prior_step_0"):
        prior = grow(prior, n, steps[0])
    with jax.named_scope("span_step_0"):
        span = grow(kv, n, span_steps[0])
    normed = after(normed, prior, span)
    with jax.named_scope("weights_step"):
        w_near = lax.ppermute(w_send, "head", [(0, 1), (1, 0)])
        w_far = swap(w_near, n, 1)
    q, own_bias, span_bias = pl.pallas_call(
        query_kernel,
        out_shape=[
            jax.ShapeDtypeStruct((2 * blocks * group * BLOCK, 256), BF16),
            jax.ShapeDtypeStruct((rows, rows), F32),
            jax.ShapeDtypeStruct((blocks, n * PAGE), F32),
        ],
        in_specs=[spec(VMEM)] * 3 + [spec(pltpu.HBM)] * 5,
        out_specs=[spec(VMEM)] * 3,
        scratch_shapes=[
            VMEM(w_query.shape, BF16),
            VMEM((1, head_dim), F32),
            SMEM(span_order.shape, jnp.int32),
            SMEM(key_live.shape, jnp.int32),
            SMEM((masks.size,), jnp.int32),
            pltpu.SemaphoreType.DMA((4,)),
            pltpu.SemaphoreType.DMA((w_query.shape[1] // 256,)),
        ],
        compiler_params=params(),
        cost_estimate=cost(2 * rows * width * 512, 4 << 20),
    )(
        normed,
        cosine,
        sine,
        *in_hbm(w_query, query_gain.reshape(1, -1), span_order, key_live, jnp.asarray(masks)),
    )
    for i, step in enumerate(steps[1:-1], 1):
        with jax.named_scope(f"prior_step_{i}"):
            prior = grow(prior, n, step)
        with jax.named_scope(f"span_step_{i}"):
            span = grow(span, n, span_steps[i])
    prior, span, _ = lax.optimization_barrier((prior, span, q))
    with jax.named_scope("prior_last"):
        prior_far = swap(prior, n, steps[-1])
    with jax.named_scope("span_last"):
        span_far = swap(span, n, span_steps[-1])
    prior, span = after(prior, own_bias), after(span, own_bias)
    half = prior.shape[0] // 2
    with jax.named_scope("prior_core_near"):
        prior_core = [swap(prior[:half], n, 1), swap(prior[half:], n, 1)]
    with jax.named_scope("span_core_near"):
        span_core = [swap(span[:half], n, 1), swap(span[half:], n, 1)]

    common = dict(bias=span_bias, blocks=blocks, group=group)
    part = n // 4 * PAGE
    chunks = [(prior, None), (span, 0)]
    state = attention(q, (kv, own_bias), chunks, state=None, last=False, **common)
    chunks = [(c, None) for c in prior_core]
    chunks += [(c, 2 * part + i * half) for i, c in enumerate(span_core)]
    state = attention(q, None, chunks, state=state, last=False, join=2, **common)
    prior_far, span_far, *state = lax.optimization_barrier((prior_far, span_far, *state))
    with jax.named_scope("core_far"):
        far_core = swap(jnp.concatenate([prior_far, span_far], axis=0), n, 1)
    chunks = [(prior_far, None), (span_far, part)]
    state = attention(q, None, chunks, state=state, last=False, **common)
    chunks = [(far_core, (None, 3 * part))]
    heads = attention(q, None, chunks, state=state, last=True, **common)
    peer = lax.ppermute(heads, "head", [(0, 1), (1, 0)])

    all_span = [span, span_far, *span_core, far_core]
    new_keys, new_values, partial = pl.pallas_call(
        functools.partial(pages_kernel, len(all_span)),
        out_shape=[jax.ShapeDtypeStruct((1, PAGE, 128), BF16)] * 2
        + [jax.ShapeDtypeStruct((rows, out_width), F32)],
        in_specs=[spec(SMEM)] * 3 + [spec(VMEM), spec(pltpu.HBM)] + [spec(pl.ANY)] * len(all_span),
        out_specs=[spec(VMEM)] * 3,
        scratch_shapes=[
            VMEM((w_output.shape[0], out_width), BF16),
            pltpu.SemaphoreType.DMA((2,)),
            pltpu.SemaphoreType.DMA((w_output.shape[0] // 64,)),
        ],
        compiler_params=params(),
        cost_estimate=cost(2 * rows * 512 * out_width, 1 << 21),
    )(page_dest, span_order, jnp.asarray(where), heads, *in_hbm(w_output), *all_span)

    attn_out = pl.pallas_call(
        project_kernel,
        out_shape=jax.ShapeDtypeStruct((rows, out_width), F32),
        in_specs=[spec(VMEM)] * 4,
        out_specs=spec(VMEM),
        compiler_params=params(),
        cost_estimate=cost(2 * rows * 512 * out_width, 2 << 20),
    )(partial, peer, w_near, w_far)
    return attn_out, new_keys, new_values


def solution(mesh):
    return jax.shard_map(
        functools.partial(body, mesh.shape["seq"]),
        mesh=mesh,
        in_specs=(
            P("seq", None),
            P(),
            P(None, "head"),
            P(None, "head"),
            P(None, "head"),
            P(),
            P(),
            P("head", None),
            P("seq", None, "head"),
            P("seq", None, "head"),
            P(),
            P(),
            P(),
            P(),
        ),
        out_specs=(P("seq", "head"), P("seq", None, "head"), P("seq", None, "head")),
        check_vma=False,
    )
```
